256 devices in a mesh: grp: 8 (over z_lo, y), tile: 32 (over x, z_hi, core).
Axes of the slice: x: 4, y: 4, z: 8 (z_hi: 4, z_lo: 2; z = z_hi * 2 + z_lo), core: 2. Of those that a mesh axis runs over, the one named last changes fastest.
Arguments:
- latent: bfloat16 [256, 2, 32, 32, 512], P(('grp', 'tile')), parts along dimension 0
- lengths: int32 [16], P('grp'), parts along dimension 0, may hold values from 1 to 2, as said below
- tile_of_slot: int32 [256], P('grp'), parts along dimension 0, may hold values from 0 to 31, each once
- norm_gain: float32 [512], replicated, may hold values from 0.5 to 1.5
- norm_shift: float32 [512], replicated, may hold values from -3 to 3
- conv_weight: bfloat16 [3, 3, 3, 512, 256], replicated, may hold values from -0.0546875 to 0.0546875
- conv_bias: float32 [256], replicated, may hold values from -3 to 3
Outputs:
- decoded: bfloat16 [256, 2, 32, 32, 256], P(('grp', 'tile')), parts along dimension 0
The draws below stay inside these ranges and needn't reach their ends.
There are 8 independent parts, one for each index of `grp`. The reference program is written for one: setup_inputs(seed, part) draws one part's arguments, and reference() takes and returns one part's arrays. A program takes and returns all parts, laid end to end along the dimension named above; an argument that names none is the same for every part. Nothing has to cross between parts.
Inputs may be any that keep to these rules, and one draw needn't show every extreme that they name: `lengths`: one of the two videos has all 2 frames, the other fewer.
All inputs are finite; a program needn't handle non-finite values.
Results may differ from the reference program's by a relative error of at most 0.0044.
Values may be sent and summed in bfloat16 or wider, within the bound.
A program may use at most 128 MiB of HBM per device.

```python
import math
import jax
import jax.numpy as jnp
from jax import lax

C = 512
CO = 256
GROUPS = 32
F = 2
HT = 32
WT = 32
TX = 4
TILES = 32
TY = 4
CG = 16


def draw_latent(key, part):
    key = jax.random.fold_in(key, 11)
    first, second, third = jax.random.split(key, 3)
    shape = (TILES, F, HT, WT, C)
    base = jax.random.normal(first, shape, jnp.float32)
    rows = jnp.exp(jax.random.uniform(second, (TILES, F, HT, 1, 1), jnp.float32, 0.0, math.log(10.0)))
    chans = jnp.exp(jax.random.uniform(third, (C,), jnp.float32, 0.0, math.log(3.0)))
    slots = jnp.exp(math.log(3.0) * jnp.arange(TILES, dtype=jnp.float32) / (TILES - 1))
    return (base * rows * chans * slots[:, None, None, None, None] * 0.25).astype(jnp.bfloat16)


def draw_lengths(key, part):
    key = jax.random.fold_in(key, 5)
    first, second = jax.random.split(key)
    shorter = jax.random.randint(first, (), 1, F)
    fuller = jax.random.randint(second, (), 0, 2)
    return jnp.where(jnp.arange(2, dtype=jnp.int32) == fuller, F, shorter).astype(jnp.int32)


def gaussian(stream_key, dims, spread, bound, held_as=jnp.bfloat16):
    return jnp.clip(spread * jax.random.normal(stream_key, dims, jnp.float32), -bound, bound).astype(held_as)


def setup_inputs(seed: int = 0, part: int = 0) -> dict:
    arg_keys = jax.random.split(jax.random.key(seed), 8)
    part_splits = jax.random.split(jax.random.fold_in(arg_keys[7], part), 8)
    latent = draw_latent(jax.random.fold_in(jax.random.fold_in(arg_keys[7], part), 71), part)
    lengths = draw_lengths(jax.random.fold_in(jax.random.fold_in(arg_keys[7], part), 71), part)
    tile_of_slot = jax.random.permutation(part_splits[2], TILES).astype(jnp.int32)
    norm_gain = jnp.clip(jax.random.uniform(arg_keys[3], (C,), jnp.float32, 0.5, 1.5), 0.5, 1.5)
    norm_shift = gaussian(arg_keys[4], (C,), 0.5, 3.0, jnp.float32)
    conv_weight = gaussian(arg_keys[5], (3, 3, 3, C, CO), (27 * C) ** -0.5, 0.0546875)
    conv_bias = gaussian(arg_keys[6], (CO,), 0.5, 3.0, jnp.float32)
    return dict(latent=latent, lengths=lengths, tile_of_slot=tile_of_slot, norm_gain=norm_gain, norm_shift=norm_shift, conv_weight=conv_weight, conv_bias=conv_bias)


def reference(latent, lengths, tile_of_slot, norm_gain, norm_shift, conv_weight, conv_bias):
    slot_ids = jnp.arange(TILES, dtype=jnp.int32)
    slot_of_tile = jnp.zeros((TILES,), jnp.int32).at[tile_of_slot].set(slot_ids)
    ordered = latent[slot_of_tile]
    height = TY * HT
    width = TX * WT
    video = ordered.reshape(2, TY, TX, F, HT, WT, C).transpose(0, 3, 1, 4, 2, 5, 6).reshape(2, F, height, width, C).astype(jnp.float32)
    frame_mask = (jnp.arange(F, dtype=jnp.int32)[None, :] < lengths[:, None]).astype(jnp.float32)
    masked = video * frame_mask[:, :, None, None, None]
    sums = lax.optimization_barrier(jnp.sum(masked, axis=(1, 2, 3))).reshape(2, GROUPS, CG).sum(-1)
    squares = lax.optimization_barrier(jnp.sum(masked * video, axis=(1, 2, 3))).reshape(2, GROUPS, CG).sum(-1)
    count = (lengths.astype(jnp.float32) * float(height * width * CG))[:, None]
    mean = sums / count
    inv = 1.0 / jnp.sqrt(squares / count - mean * mean + 1e-06)
    chan_mean = jnp.repeat(mean, CG, axis=1)
    chan_inv = jnp.repeat(inv, CG, axis=1)
    normed = (video - chan_mean[:, None, None, None, :]) * chan_inv[:, None, None, None, :] * norm_gain + norm_shift
    hidden = jax.nn.silu(normed).astype(jnp.bfloat16)
    hidden = jnp.concatenate([hidden[:, :1], hidden[:, :1], hidden], axis=1)
    padded = jnp.pad(hidden, ((0, 0), (0, 0), (1, 1), (1, 1), (0, 0)))

    def convolve(single):
        total = jnp.zeros((F * height * width, CO), jnp.float32)
        for depth in range(3):
            for row_off in range(3):
                for col_off in range(3):
                    window = single[depth:depth + F, row_off:row_off + height, col_off:col_off + width].reshape(-1, C)
                    total = total + jnp.dot(window, conv_weight[depth, row_off, col_off], preferred_element_type=jnp.float32)
        return total.reshape(F, height, width, CO)
    conv = lax.map(convolve, padded) + conv_bias
    conv = conv * frame_mask[:, :, None, None, None]
    tiled = conv.astype(jnp.bfloat16).reshape(2, F, TY, HT, TX, WT, CO).transpose(0, 2, 4, 1, 3, 5, 6).reshape(TILES, F, HT, WT, CO)
    return tiled[tile_of_slot]
```

```python
import functools

import jax
import jax.numpy as jnp
from jax import lax
from jax.experimental import pallas as pl
from jax.experimental.pallas import tpu as pltpu
from jax.sharding import PartitionSpec as P

MESH = pl.DeviceIdType.MESH
F32 = jnp.float32
BF16 = jnp.bfloat16
GROUPS = 32
N = 32
ROWS = 32
COLS = 32
C = 512
CO = 256
CG = C // GROUPS
PER_VIDEO = 16
TX = 4
TY = 4
COUNT = float(TY * ROWS * TX * COLS * CG)
CHUNK = 8


def iota(shape, dim):
    return lax.broadcasted_iota(jnp.int32, shape, dim)


def exact_dot(a, b):
    return jnp.dot(a, b, precision=lax.Precision.HIGHEST, preferred_element_type=F32)


def dot(a, b):
    return jnp.dot(a, b, preferred_element_type=F32)


def activate(x, mean, scale, shift):
    y = (x - mean) * scale + shift
    half = 0.5 * y
    return (half + half * jnp.tanh(half)).astype(BF16).astype(F32)


def kernel(
    lat_hbm, w_hbm, tos_s, len_s, tos_v, gain_ref, shift_ref, bias_ref, out_ref,
    lat, w, wa, hp, acc, send1, recv1, send2, recv2, stat, srecv, norm, edge, pick,
    lat_sem, w_sem, ssem, rsem,
):
    me = lax.axis_index("tile")
    grp = lax.axis_index("grp")

    def other(k):
        return lax.rem(me + k, N)

    barrier = pltpu.get_barrier_semaphore()

    def greet(k, carry):
        pl.semaphore_signal(barrier, inc=1, device_id=(grp, other(k)), device_id_type=MESH)
        return carry

    lax.fori_loop(1, N, greet, 0)
    lat_copy = pltpu.make_async_copy(lat_hbm, lat, lat_sem)
    lat_copy.start()
    w_copy = pltpu.make_async_copy(w_hbm, w, w_sem)
    w_copy.start()

    def send(phase, src, dst, by_target):
        def one(k, carry):
            to = other(k)
            pltpu.make_async_remote_copy(
                src_ref=src.at[to] if by_target else src,
                dst_ref=dst.at[me],
                send_sem=ssem.at[phase],
                recv_sem=rsem.at[phase],
                device_id=(grp, to),
                device_id_type=MESH,
            ).start()
            return carry

        lax.fori_loop(1, N, one, 0)

    def whole(phase, dst):
        part = dst.at[pl.ds(0, N - 1)]
        return pltpu.make_async_remote_copy(
            src_ref=part, dst_ref=part, send_sem=ssem.at[phase], recv_sem=rsem.at[phase],
            device_id=(grp, other(1)), device_id_type=MESH,
        )

    my_tile = tos_s[me]
    my_second = my_tile >= PER_VIDEO
    my_length = jnp.where(my_second, len_s[1], len_s[0])
    valid = [jnp.where(my_length > f, 1.0, 0.0).astype(F32) for f in range(2)]

    lat_copy.wait()
    total = jnp.zeros((1, C), F32)
    squares = jnp.zeros((1, C), F32)
    for f in range(2):

        def row_sums(r, carry):
            s, q = carry
            x = lat[f, r].astype(F32)
            return s + x, q + x * x

        zero = jnp.zeros((COLS, C), F32)
        s, q = lax.fori_loop(0, ROWS, row_sums, (zero, zero))
        total = total + valid[f] * jnp.sum(s, axis=0, keepdims=True)
        squares = squares + valid[f] * jnp.sum(q, axis=0, keepdims=True)
    chan, lane = iota((C, 128), 0), iota((C, 128), 1)
    to_sum = jnp.where(chan // CG == lane, 1.0, 0.0).astype(F32)
    to_square = jnp.where(chan // CG + GROUPS == lane, 1.0, 0.0).astype(F32)
    packed = exact_dot(jnp.broadcast_to(total, (8, C)), to_sum) + exact_dot(
        jnp.broadcast_to(squares, (8, C)), to_square
    )
    stat[...] = packed[0:1]

    sub = iota((8, C), 0)

    def edge_rows(f, e, p):
        if e < 2:
            return lat[f, 0 if e == 0 else ROWS - 1, 8 * p : 8 * p + 8].astype(F32)
        found = jnp.zeros((8, C), F32)
        for q in range(8):
            if e == 2:
                block = lat[f, 8 * p + q, 0:16].astype(F32)[0:8]
                turned = pltpu.roll(block, q, 0) if q else block
            else:
                block = lat[f, 8 * p + q, 16:32].astype(F32)[8:16]
                turned = pltpu.roll(block, q + 1, 0) if q < 7 else block
            found = jnp.where(sub == q, turned, found)
        return found

    def fold(x):
        return jnp.concatenate([x[:, : C // 2], x[:, C // 2 :]], axis=0).astype(BF16)

    for e in range(4):
        for p in range(4):
            first, second = edge_rows(0, e, p), edge_rows(1, e, p)
            send1[e * 8 + 2 * p] = fold(jnp.where(sub < 4, first, pltpu.roll(second, 4, 0)))
            send1[e * 8 + 2 * p + 1] = fold(jnp.where(sub < 4, pltpu.roll(first, 4, 0), second))

    pl.semaphore_wait(barrier, N - 1)
    send(0, stat, srecv, False)
    send(1, send1, recv1, True)
    srecv[me] = stat[...]
    recv1[me] = send1[me]

    kind = me // 8
    part = lax.rem(me, 8)
    tos_row = tos_v[...].astype(F32)
    owner = iota((N * 8, N), 0) // 8
    tile_here = jnp.sum(
        jnp.where(owner == iota((N * 8, N), 1), jnp.broadcast_to(tos_row, (N * 8, N)), 0.0),
        axis=1, keepdims=True,
    ).astype(jnp.int32)
    expand = jnp.where(iota((N, N * 8), 0) == iota((N, N * 8), 1) // 8, 1.0, 0.0).astype(F32)
    tile_there = exact_dot(jnp.broadcast_to(tos_row, (8, N)), expand)[0:1].astype(jnp.int32)
    row_step = jnp.where(kind == 0, 1, jnp.where(kind == 1, -1, 0))
    col_step = jnp.where(kind == 2, 1, jnp.where(kind == 3, -1, 0))
    px = lax.rem(iota((N * 8, 1), 0), 4)
    same_row = lax.rem(iota((N * 8, N * 8), 0), 8) == lax.rem(iota((N * 8, N * 8), 1), 8)
    video = tile_here // PER_VIDEO
    tile_row = lax.rem(tile_here, PER_VIDEO) // TX
    tile_col = lax.rem(tile_here, TX)
    low_end = jnp.where((px == 0) & (part == 0), 1, 0)
    high_end = jnp.where((px == 3) & (part == 7), 1, 0)
    for side in range(2):
        near_row = tile_row + row_step
        near_col = tile_col + col_step
        if side == 1:
            turn = jnp.where(kind < 2, 1, 100)
            near_col = near_col + turn * low_end - turn * high_end
        inside = (near_row >= 0) & (near_row < TY) & (near_col >= 0) & (near_col < TX)
        near = jnp.where(inside, video * PER_VIDEO + near_row * TX + near_col, -1)
        pick[side] = jnp.where((near == tile_there) & same_row, 1.0, 0.0).astype(BF16)

    w_copy.wait()

    def add_weights(i, carry):
        tap, at = i // 4, pl.multiple_of(lax.rem(i, 4) * 128, 128)
        rows = pl.ds(at, 128)
        whole_sum = (
            w[tap, rows].astype(F32) + w[9 + tap, rows].astype(F32) + w[18 + tap, rows].astype(F32)
        )
        wa[tap, rows] = whole_sum.astype(BF16)
        return carry

    lax.fori_loop(0, 36, add_weights, 0)
    for u in range(2):
        hp[u, 0] = jnp.zeros((COLS, C), BF16)
        hp[u, ROWS + 1] = jnp.zeros((COLS, C), BF16)

    whole(0, srecv).wait_recv()
    sums = [jnp.zeros((1, 128), F32), jnp.zeros((1, 128), F32)]
    for s in range(N):
        row = srecv[s]
        second = jnp.where(tos_s[s] >= PER_VIDEO, 1.0, 0.0).astype(F32)
        sums = [sums[0] + row * (1.0 - second), sums[1] + row * second]
    lane, chan = iota((128, C), 0), iota((128, C), 1)
    from_sum = jnp.where(chan // CG == lane, 1.0, 0.0).astype(F32)
    from_square = jnp.where(chan // CG + GROUPS == lane, 1.0, 0.0).astype(F32)
    for v in range(2):
        count = len_s[v].astype(F32) * COUNT
        spread = jnp.broadcast_to(sums[v], (8, 128))
        mean = exact_dot(spread, from_sum) / count
        square = exact_dot(spread, from_square) / count
        norm[v, 0] = mean
        norm[v, 1] = (1.0 / jnp.sqrt(square - mean * mean + 1e-06)) * gain_ref[...]
    shift8 = jnp.broadcast_to(shift_ref[...], (8, C))

    def halves(x):
        return jnp.concatenate([x[:, : C // 2], x[:, C // 2 :]], axis=0)

    shift16 = halves(shift8)
    half_sub = iota((8, C // 2), 0)
    whole(1, recv1).wait_recv()

    def chunk_rows(p, carry):
        parts = [[], []]
        for j in range(2):
            s = 2 * p + j
            v = jnp.where(tos_s[s] >= PER_VIDEO, 1, 0)
            h = activate(recv1[s].astype(F32), halves(norm[v, 0]), halves(norm[v, 1]), shift16)
            for half in range(2):
                x = h[8 * half : 8 * half + 8]
                parts[half].append(jnp.where(half_sub < 4, x, x - pltpu.roll(x, 4, 0)))
        for half in range(2):
            edge[half, pl.ds(pl.multiple_of(16 * p, 16), 16)] = jnp.concatenate(
                parts[half], axis=0
            ).astype(BF16)
        return carry

    lax.fori_loop(0, N // 2, chunk_rows, 0)
    base = jnp.where(kind == 0, 6, jnp.where(kind == 2, 2, 0))
    stride = jnp.where(kind < 2, 1, 3)
    row8 = lax.rem(iota((N * 8, CO), 0), 8)
    px = lax.rem(row8, 4)
    half_c = C // 2
    taps = []
    for t in range(3):
        tap = base + stride * t
        ya = dot(edge[0], wa[tap, :half_c]) + dot(edge[1], wa[tap, half_c:])
        yc = dot(edge[0], w[18 + tap, :half_c]) + dot(edge[1], w[18 + tap, half_c:])
        taps.append(jnp.where(row8 < 4, ya, yc))
    main = (
        taps[1]
        + jnp.where(px >= 1, pltpu.roll(taps[0], 1, 0), 0.0)
        + jnp.where(px <= 2, pltpu.roll(taps[2], N * 8 - 1, 0), 0.0)
    )
    extra = jnp.where(px == 3, taps[0], jnp.where(px == 0, taps[2], 0.0))
    main = dot(pick[0], main.astype(BF16)).reshape(N, 8, CO)
    extra = dot(pick[1], extra.astype(BF16)).reshape(N, 8, CO)
    send2[...] = jnp.concatenate([main, extra], axis=1).astype(BF16)
    send(2, send2, recv2, True)
    recv2[me] = send2[me]

    mine = jnp.where(my_second, 1, 0)
    mean = jnp.concatenate([norm[mine, 0]] * 4, axis=0)
    scale = jnp.concatenate([norm[mine, 1]] * 4, axis=0)
    shift = jnp.concatenate([shift8] * 4, axis=0)

    def hidden_row(r, carry):
        first = activate(lat[0, r].astype(F32), mean, scale, shift)
        second = activate(lat[1, r].astype(F32), mean, scale, shift)
        hp[0, r + 1] = first.astype(BF16)
        hp[1, r + 1] = (second - first).astype(BF16)
        return carry

    lax.fori_loop(0, ROWS, hidden_row, 0)
    col = lax.rem(iota((CHUNK * COLS, CO), 0), COLS)
    for u in range(2):

        def conv_rows(i, carry):
            r0 = i * CHUNK
            parts = []
            for c in range(3):
                part_sum = None
                for b in range(3):
                    window = hp[u, pl.ds(r0 + b, CHUNK)].reshape(CHUNK * COLS, C)
                    weight = wa[3 * b + c] if u == 0 else w[18 + 3 * b + c]
                    product = dot(window, weight)
                    part_sum = product if part_sum is None else part_sum + product
                parts.append(part_sum)
            result = (
                parts[1]
                + jnp.where(col > 0, pltpu.roll(parts[0], 1, 0), 0.0)
                + jnp.where(col < COLS - 1, pltpu.roll(parts[2], CHUNK * COLS - 1, 0), 0.0)
            )
            acc[u, pl.ds(r0, CHUNK)] = result.reshape(CHUNK, COLS, CO)
            return carry

        lax.fori_loop(0, ROWS // CHUNK, conv_rows, 0)

    whole(2, recv2).wait_recv()

    def hits(shape, unit, pos):
        at = iota(shape, 1)
        g, r = at // 16, lax.rem(at, 16)
        from_px = lax.rem(r, 4)
        lands = jnp.where(
            r < 8,
            4 * g + from_px,
            jnp.where(
                from_px == 0,
                lax.rem(4 * g + 31, 32),
                jnp.where(from_px == 3, lax.rem(4 * g + 4, 32), -1),
            ),
        )
        return (lax.rem(r, 8) // 4 == unit) & (lands == pos)

    line_at = iota((64, 128), 0)
    to_line = jnp.where(hits((64, 128), line_at // 32, lax.rem(line_at, 32)), 1.0, 0.0).astype(BF16)
    for e, row in ((0, ROWS - 1), (1, 0)):
        line = dot(to_line, recv2[8 * e : 8 * e + 8].reshape(128, CO))
        acc[0, row] += line[:COLS]
        acc[1, row] += line[COLS:]
    side_at = iota((512, 128), 0)
    on_side = hits((512, 128), side_at // 256, lax.rem(side_at, 256) // 8)
    for e, at in ((2, COLS - 8), (3, 0)):
        to_side = jnp.where(on_side & (lax.rem(side_at, 8) == (7 if e == 2 else 0)), 1.0, 0.0)
        side = dot(to_side.astype(BF16), recv2[8 * e : 8 * e + 8].reshape(128, CO))
        side = side.reshape(2, ROWS, 8, CO)
        for u in range(2):
            acc[u, :, at : at + 8] += side[u]

    bias = jnp.broadcast_to(bias_ref[...], (COLS, CO))

    def finish(r, carry):
        first = acc[0, r] + bias
        out_ref[0, r] = (first * valid[0]).astype(BF16)
        out_ref[1, r] = ((first + acc[1, r]) * valid[1]).astype(BF16)
        return carry

    lax.fori_loop(0, ROWS, finish, 0)
    whole(0, srecv).wait_send()
    whole(1, recv1).wait_send()
    whole(2, recv2).wait_send()


def body(latent, lengths, tile_of_slot, norm_gain, norm_shift, conv_weight, conv_bias):
    vmem = pl.BlockSpec(memory_space=pltpu.VMEM)
    smem = pl.BlockSpec(memory_space=pltpu.SMEM)
    anywhere = pl.BlockSpec(memory_space=pl.ANY)
    decoded = pl.pallas_call(
        kernel,
        out_shape=jax.ShapeDtypeStruct((2, ROWS, COLS, CO), BF16),
        in_specs=[anywhere, anywhere, smem, smem, vmem, vmem, vmem, vmem],
        out_specs=vmem,
        scratch_shapes=[
            pltpu.VMEM((2, ROWS, COLS, C), BF16),
            pltpu.VMEM((27, C, CO), BF16),
            pltpu.VMEM((9, C, CO), BF16),
            pltpu.VMEM((2, ROWS + 2, COLS, C), BF16),
            pltpu.VMEM((2, ROWS, COLS, CO), F32),
            pltpu.VMEM((N, 16, C // 2), BF16),
            pltpu.VMEM((N, 16, C // 2), BF16),
            pltpu.VMEM((N, 16, CO), BF16),
            pltpu.VMEM((N, 16, CO), BF16),
            pltpu.VMEM((1, 128), F32),
            pltpu.VMEM((N, 1, 128), F32),
            pltpu.VMEM((2, 2, 8, C), F32),
            pltpu.VMEM((2, N * 8, C // 2), BF16),
            pltpu.VMEM((2, N * 8, N * 8), BF16),
            pltpu.SemaphoreType.DMA(()),
            pltpu.SemaphoreType.DMA(()),
            pltpu.SemaphoreType.DMA((3,)),
            pltpu.SemaphoreType.DMA((3,)),
        ],
        compiler_params=pltpu.CompilerParams(
            collective_id=0, has_side_effects=True, vmem_limit_bytes=48 << 20
        ),
    )(
        latent[0],
        conv_weight.reshape(27, C, CO),
        tile_of_slot,
        lengths,
        tile_of_slot.reshape(1, N),
        norm_gain.reshape(1, C),
        norm_shift.reshape(1, C),
        conv_bias.reshape(1, CO),
    )
    return decoded[None]


def solution(mesh):
    placed = (P(("grp", "tile"), None, None, None, None), P("grp"), P("grp"), P(), P(), P(), P())
    return jax.shard_map(
        body,
        mesh=mesh,
        in_specs=placed,
        out_specs=P(("grp", "tile"), None, None, None, None),
        check_vma=False,
    )
```

```python
import functools

import jax
import jax.numpy as jnp
from jax import lax
from jax.experimental import pallas as pl
from jax.experimental.pallas import tpu as pltpu
from jax.sharding import PartitionSpec as P

MESH = pl.DeviceIdType.MESH
F32 = jnp.float32
BF16 = jnp.bfloat16
GROUPS = 32
N = 32
ROWS = 32
COLS = 32
C = 512
CO = 256
CG = C // GROUPS
PER_VIDEO = 16
TX = 4
TY = 4
COUNT = float(TY * ROWS * TX * COLS * CG)
CHUNK = 16
EARLY = 0


def iota(shape, dim):
    return lax.broadcasted_iota(jnp.int32, shape, dim)


def exact_dot(a, b):
    return jnp.dot(a, b, precision=lax.Precision.HIGHEST, preferred_element_type=F32)


def dot(a, b):
    return jnp.dot(a, b, preferred_element_type=F32)


def activate(x, mean, scale, shift):
    y = (x - mean) * scale + shift
    half = 0.5 * y
    return (half + half * jnp.tanh(half)).astype(BF16).astype(F32)


def kernel(
    lat_hbm, w_hbm, tos_hbm, len_hbm, tos_row_hbm, gain_hbm, shift_hbm, bias_hbm, out_ref,
    lat, w, wa, hp, acc, send1, recv1, send2, recv2, stat, srecv, norm, norm16, edge, pick,
    tos_s, len_s, tos_v, gain_ref, shift_ref, bias_ref,
    lat_sem, w_sem, small_sem, ssem, rsem,
):
    me = lax.axis_index("tile")
    grp = lax.axis_index("grp")
    my_x, my_z, my_core = me // 8, lax.rem(me // 2, 4), lax.rem(me, 2)

    def to_all(planes, action, xs=None):
        xs = xs or [lax.rem(my_x + 2 + j, 4) * 8 for j in range(4)]
        cores = [my_core, 1 - my_core]
        for plane in planes:
            for x in xs:
                for core in cores:
                    to = x + plane * 2 + core
                    pl.when(to != me)(functools.partial(action, to))

    by_distance = (
        lax.rem(my_z + 2, 4), 3 - my_z, my_z + 1 - 2 * lax.rem(my_z, 2), my_z
    )
    barrier = pltpu.get_barrier_semaphore()

    def greet(to):
        pl.semaphore_signal(barrier, inc=1, device_id=(grp, to), device_id_type=MESH)

    to_all(by_distance, greet)
    lat_copy = pltpu.make_async_copy(lat_hbm, lat, lat_sem)
    lat_copy.start()
    w_copy = pltpu.make_async_copy(w_hbm, w, w_sem)
    w_copy.start()

    small = [
        pltpu.make_async_copy(src, dst, small_sem.at[i])
        for i, (src, dst) in enumerate(
            (
                (tos_hbm, tos_s), (len_hbm, len_s), (tos_row_hbm, tos_v),
                (gain_hbm, gain_ref), (shift_hbm, shift_ref), (bias_hbm, bias_ref),
            )
        )
    ]
    for copy in small:
        copy.start()

    def send(phase, src, dst, to):
        pltpu.make_async_remote_copy(
            src_ref=src, dst_ref=dst.at[me], send_sem=ssem.at[phase], recv_sem=rsem.at[phase],
            device_id=(grp, to), device_id_type=MESH,
        ).start()

    def whole(phase, dst):
        part = dst.at[pl.ds(0, N - 1)]
        return pltpu.make_async_remote_copy(
            src_ref=part, dst_ref=part, send_sem=ssem.at[phase], recv_sem=rsem.at[phase],
            device_id=(grp, lax.rem(me + 1, N)), device_id_type=MESH,
        )

    for copy in small:
        copy.wait()
    my_tile = tos_s[me]
    my_second = my_tile >= PER_VIDEO
    my_length = jnp.where(my_second, len_s[1], len_s[0])
    valid = [jnp.where(my_length > f, 1.0, 0.0).astype(F32) for f in range(2)]

    lat_copy.wait()
    total = jnp.zeros((1, C), F32)
    squares = jnp.zeros((1, C), F32)
    for f in range(2):

        def row_sums(r, carry):
            s, q = carry
            x = lat[f, r].astype(F32)
            return s + x, q + x * x

        zero = jnp.zeros((COLS, C), F32)
        s, q = lax.fori_loop(0, ROWS, row_sums, (zero, zero))
        total = total + valid[f] * jnp.sum(s, axis=0, keepdims=True)
        squares = squares + valid[f] * jnp.sum(q, axis=0, keepdims=True)
    chan, lane = iota((C, 128), 0), iota((C, 128), 1)
    to_sum = jnp.where(chan // CG == lane, 1.0, 0.0).astype(F32)
    to_square = jnp.where(chan // CG + GROUPS == lane, 1.0, 0.0).astype(F32)
    packed = exact_dot(jnp.broadcast_to(total, (8, C)), to_sum) + exact_dot(
        jnp.broadcast_to(squares, (8, C)), to_square
    )
    stat[...] = packed[0:1]

    sub = iota((8, C), 0)

    def edge_rows(f, e, p):
        if e < 2:
            return lat[f, 0 if e == 0 else ROWS - 1, 8 * p : 8 * p + 8].astype(F32)
        found = jnp.zeros((8, C), F32)
        for q in range(8):
            if e == 2:
                block = lat[f, 8 * p + q, 0:16].astype(F32)[0:8]
                turned = pltpu.roll(block, q, 0) if q else block
            else:
                block = lat[f, 8 * p + q, 16:32].astype(F32)[8:16]
                turned = pltpu.roll(block, q + 1, 0) if q < 7 else block
            found = jnp.where(sub == q, turned, found)
        return found

    def quads(x, y):
        turned = pltpu.roll(x, 4, 0), pltpu.roll(y, 4, 0)
        top = sub[:, :128] < 4
        return jnp.where(top, x, turned[1]), jnp.where(top, turned[0], y)

    def lanes(x):
        return [x[:, 128 * q : 128 * (q + 1)] for q in range(4)]

    for f in range(2):
        for e in range(4):
            for p in range(4):
                q = lanes(edge_rows(f, e, p))
                front, back = quads(q[0], q[1]), quads(q[2], q[3])
                for i in range(2):
                    send1[f, e * 8 + 2 * p + i] = jnp.concatenate(
                        [front[i], back[i]], axis=0
                    ).astype(BF16)

    pl.semaphore_wait(barrier, N - 1)

    to_all(by_distance, lambda to: send(0, stat, srecv, to))
    to_all(by_distance, lambda to: send(1, send1.at[0, to], recv1.at[0], to))
    to_all(by_distance, lambda to: send(2, send1.at[1, to], recv1.at[1], to))
    srecv[me] = stat[...]
    for f in range(2):
        recv1[f, me] = send1[f, me]

    kind = me // 8
    part = lax.rem(me, 8)
    tos_row = tos_v[...].astype(F32)
    owner = iota((N * 8, N), 0) // 8
    tile_here = jnp.sum(
        jnp.where(owner == iota((N * 8, N), 1), jnp.broadcast_to(tos_row, (N * 8, N)), 0.0),
        axis=1, keepdims=True,
    ).astype(jnp.int32)
    expand = jnp.where(
        iota((N, N * 8), 0) == lax.rem(iota((N, N * 8), 1) // 4, N), 1.0, 0.0
    ).astype(F32)
    tile_there = exact_dot(jnp.broadcast_to(tos_row, (8, N)), expand)[0:1].astype(jnp.int32)
    row_step = jnp.where(kind == 0, 1, jnp.where(kind == 1, -1, 0))
    col_step = jnp.where(kind == 2, 1, jnp.where(kind == 3, -1, 0))
    line8 = lax.rem(iota((N * 8, 1), 0), 8)
    turn = jnp.where(kind < 2, 1, 100)
    low_end = jnp.where((line8 == 4) & (part == 0), turn, 0)
    high_end = jnp.where((line8 == 7) & (part == 7), turn, 0)
    near_row = lax.rem(tile_here, PER_VIDEO) // TX + row_step
    near_col = lax.rem(tile_here, TX) + col_step + low_end - high_end
    inside = (near_row >= 0) & (near_row < TY) & (near_col >= 0) & (near_col < TX)
    near = jnp.where(
        inside, tile_here // PER_VIDEO * PER_VIDEO + near_row * TX + near_col, -1
    )
    there = iota((N * 8, N * 8), 1)
    same_line = lax.rem(iota((N * 8, N * 8), 0), 8) == there // (4 * N) * 4 + lax.rem(there, 4)
    pick[...] = jnp.where((near == tile_there) & same_line, 1.0, 0.0).astype(BF16)

    w_copy.wait()

    def add_weights(i, carry):
        tap, at = i // 4, pl.multiple_of(lax.rem(i, 4) * 128, 128)
        rows = pl.ds(at, 128)
        whole_sum = (
            w[tap, rows].astype(F32) + w[9 + tap, rows].astype(F32) + w[18 + tap, rows].astype(F32)
        )
        wa[tap, rows] = whole_sum.astype(BF16)
        return carry

    lax.fori_loop(0, 36, add_weights, 0)
    for u in range(2):
        hp[u, 0] = jnp.zeros((COLS, C), BF16)
        hp[u, ROWS + 1] = jnp.zeros((COLS, C), BF16)

    whole(0, srecv).wait_recv()
    sums = [jnp.zeros((1, 128), F32), jnp.zeros((1, 128), F32)]
    for s in range(N):
        row = srecv[s]
        second = jnp.where(tos_s[s] >= PER_VIDEO, 1.0, 0.0).astype(F32)
        sums = [sums[0] + row * (1.0 - second), sums[1] + row * second]
    lane, chan = iota((128, C), 0), iota((128, C), 1)
    from_sum = jnp.where(chan // CG == lane, 1.0, 0.0).astype(F32)
    from_square = jnp.where(chan // CG + GROUPS == lane, 1.0, 0.0).astype(F32)
    shift8 = jnp.broadcast_to(shift_ref[...], (8, C))

    def fold(x):
        q = lanes(x)
        top = sub[:, :128] < 4
        return jnp.concatenate([jnp.where(top, q[0], q[1]), jnp.where(top, q[2], q[3])], axis=0)

    for v in range(2):
        count = len_s[v].astype(F32) * COUNT
        spread = jnp.broadcast_to(sums[v], (8, 128))
        mean = exact_dot(spread, from_sum) / count
        square = exact_dot(spread, from_square) / count
        scale = (1.0 / jnp.sqrt(square - mean * mean + 1e-06)) * gain_ref[...]
        norm[v, 0] = mean
        norm[v, 1] = scale
        norm16[v, 0] = fold(mean)
        norm16[v, 1] = fold(scale)

    mine = jnp.where(my_second, 1, 0)
    mean = jnp.concatenate([norm[mine, 0]] * 4, axis=0)
    scale = jnp.concatenate([norm[mine, 1]] * 4, axis=0)
    shift = jnp.concatenate([shift8] * 4, axis=0)

    def hidden_row(r, carry):
        first = activate(lat[0, r].astype(F32), mean, scale, shift)
        second = activate(lat[1, r].astype(F32), mean, scale, shift)
        hp[0, r + 1] = first.astype(BF16)
        hp[1, r + 1] = (second - first).astype(BF16)
        return carry

    lax.fori_loop(0, ROWS, hidden_row, 0)
    col = lax.rem(iota((CHUNK * COLS, CO), 0), COLS)

    def conv_rows(u, r0):
        parts = []
        for c in range(3):
            part_sum = None
            for b in range(3):
                window = hp[u, pl.ds(r0 + b, CHUNK)].reshape(CHUNK * COLS, C)
                weight = wa[3 * b + c] if u == 0 else w[18 + 3 * b + c]
                product = dot(window, weight)
                part_sum = product if part_sum is None else part_sum + product
            parts.append(part_sum)
        result = (
            parts[1]
            + jnp.where(col > 0, pltpu.roll(parts[0], 1, 0), 0.0)
            + jnp.where(col < COLS - 1, pltpu.roll(parts[2], CHUNK * COLS - 1, 0), 0.0)
        )
        acc[u, pl.ds(r0, CHUNK)] = result.reshape(CHUNK, COLS, CO)

    steps = [(u, r0) for u in range(2) for r0 in range(0, ROWS, CHUNK)]
    for step in steps[:EARLY]:
        conv_rows(*step)

    shift16 = fold(shift8)
    base = jnp.where(kind == 0, 6, jnp.where(kind == 2, 2, 0))
    stride = jnp.where(kind < 2, 1, 3)
    px = lax.rem(iota((N * 4, CO), 0), 4)

    def second_send(u, to):
        send(3 + u, send2.at[u, to], recv2.at[u], to)

    for u in range(2):
        whole(1 + u, recv1.at[u]).wait_recv()

        def chunk_rows(i, carry):
            rows = []
            for j in range(2):
                pair = []
                for k in range(2):
                    s = 4 * i + 2 * j + k
                    v = jnp.where(tos_s[s] >= PER_VIDEO, 1, 0)
                    pair.append(
                        activate(recv1[u, s].astype(F32), norm16[v, 0], norm16[v, 1], shift16)
                    )
                front = quads(pair[0][:8], pair[1][:8])
                back = quads(pair[0][8:], pair[1][8:])
                rows.append(jnp.concatenate([*front, *back], axis=1))
            at = pl.ds(pl.multiple_of(16 * i, 16), 16)
            rows = jnp.concatenate(rows, axis=0)
            if u == 1:
                rows = rows - edge[0, at].astype(F32)
            edge[u, at] = rows.astype(BF16)
            return carry

        lax.fori_loop(0, N // 4, chunk_rows, 0, unroll=2)
        taps = []
        for t in range(3):
            tap = base + stride * t
            taps.append(dot(edge[u], wa[tap] if u == 0 else w[18 + tap]))
        main = (
            taps[1]
            + jnp.where(px >= 1, pltpu.roll(taps[0], 1, 0), 0.0)
            + jnp.where(px <= 2, pltpu.roll(taps[2], N * 4 - 1, 0), 0.0)
        )
        extra = jnp.where(px == 3, taps[0], jnp.where(px == 0, taps[2], 0.0))
        both = jnp.concatenate([main, extra], axis=0).astype(BF16)
        picked = dot(pick[...], both).reshape(N, 8, CO)
        send2[u] = jnp.concatenate([picked[..., :128], picked[..., 128:]], axis=1).astype(BF16)
        to_all((0,), functools.partial(second_send, u), (0, 8, 16, 24))
        recv2[u, me] = send2[u, me]

    for u in range(2):
        to_all((1, 2, 3), functools.partial(second_send, u), (0, 8, 16, 24))

    for step in steps[EARLY:]:
        conv_rows(*step)

    for u in range(2):
        whole(3 + u, recv2.at[u]).wait_recv()

    def hits(shape, half, pos):
        at = iota(shape, 1)
        g, r = at // 16, lax.rem(at, 8)
        lands = jnp.where(
            r < 4,
            4 * g + r,
            jnp.where(
                r == 4,
                lax.rem(4 * g + 31, 32),
                jnp.where(r == 7, lax.rem(4 * g + 4, 32), -1),
            ),
        )
        return (lax.rem(at, 16) // 8 == half) & (lands == pos)

    def arrived(e):
        both = [recv2[u, 8 * e : 8 * e + 8].reshape(128, 128) for u in range(2)]
        return jnp.concatenate(both, axis=1)

    line_at = iota((64, 128), 0)
    to_line = jnp.where(hits((64, 128), line_at // 32, lax.rem(line_at, 32)), 1.0, 0.0).astype(BF16)
    for e, row in ((0, ROWS - 1), (1, 0)):
        line = dot(to_line, arrived(e))
        for u in range(2):
            for half in range(2):
                acc[u, row, :, 128 * half : 128 * half + 128] += line[
                    32 * half : 32 * half + 32, 128 * u : 128 * u + 128
                ]
    side_at = iota((512, 128), 0)
    on_side = hits((512, 128), side_at // 256, lax.rem(side_at, 256) // 8)
    for e, at in ((2, COLS - 8), (3, 0)):
        to_side = jnp.where(on_side & (lax.rem(side_at, 8) == (7 if e == 2 else 0)), 1.0, 0.0)
        side = dot(to_side.astype(BF16), arrived(e)).reshape(2, ROWS, 8, CO)
        for u in range(2):
            for half in range(2):
                acc[u, :, at : at + 8, 128 * half : 128 * half + 128] += side[
                    half, :, :, 128 * u : 128 * u + 128
                ]

    bias = jnp.broadcast_to(bias_ref[...], (COLS, CO))

    def finish(r, carry):
        first = acc[0, r] + bias
        out_ref[0, r] = (first * valid[0]).astype(BF16)
        out_ref[1, r] = ((first + acc[1, r]) * valid[1]).astype(BF16)
        return carry

    lax.fori_loop(0, ROWS, finish, 0)
    whole(0, srecv).wait_send()
    for u in range(2):
        whole(1 + u, recv1.at[u]).wait_send()
        whole(3 + u, recv2.at[u]).wait_send()


def body(latent, lengths, tile_of_slot, norm_gain, norm_shift, conv_weight, conv_bias):
    vmem = pl.BlockSpec(memory_space=pltpu.VMEM)
    hbm = pl.BlockSpec(memory_space=pltpu.HBM)
    decoded = pl.pallas_call(
        kernel,
        out_shape=jax.ShapeDtypeStruct((2, ROWS, COLS, CO), BF16),
        in_specs=[hbm] * 8,
        out_specs=vmem,
        scratch_shapes=[
            pltpu.VMEM((2, ROWS, COLS, C), BF16),
            pltpu.VMEM((27, C, CO), BF16),
            pltpu.VMEM((9, C, CO), BF16),
            pltpu.VMEM((2, ROWS + 2, COLS, C), BF16),
            pltpu.VMEM((2, ROWS, COLS, CO), F32),
            pltpu.VMEM((2, N, 16, 128), BF16),
            pltpu.VMEM((2, N, 16, 128), BF16),
            pltpu.VMEM((2, N, 16, 128), BF16),
            pltpu.VMEM((2, N, 16, 128), BF16),
            pltpu.VMEM((1, 128), F32),
            pltpu.VMEM((N, 1, 128), F32),
            pltpu.VMEM((2, 2, 8, C), F32),
            pltpu.VMEM((2, 2, 16, 128), F32),
            pltpu.VMEM((2, N * 4, C), BF16),
            pltpu.VMEM((N * 8, N * 8), BF16),
            pltpu.SMEM((N,), jnp.int32),
            pltpu.SMEM((2,), jnp.int32),
            pltpu.VMEM((1, N), jnp.int32),
            pltpu.VMEM((1, C), F32),
            pltpu.VMEM((1, C), F32),
            pltpu.VMEM((1, CO), F32),
            pltpu.SemaphoreType.DMA(()),
            pltpu.SemaphoreType.DMA(()),
            pltpu.SemaphoreType.DMA((6,)),
            pltpu.SemaphoreType.DMA((5,)),
            pltpu.SemaphoreType.DMA((5,)),
        ],
        compiler_params=pltpu.CompilerParams(
            collective_id=0, has_side_effects=True, vmem_limit_bytes=40 << 20
        ),
    )(
        *(
            pltpu.with_memory_space_constraint(x, pltpu.HBM)
            for x in (
                latent[0],
                conv_weight.reshape(27, C, CO),
                tile_of_slot,
                lengths,
                tile_of_slot.reshape(1, N),
                norm_gain.reshape(1, C),
                norm_shift.reshape(1, C),
                conv_bias.reshape(1, CO),
            )
        )
    )
    return decoded[None]


def solution(mesh):
    placed = (P(("grp", "tile"), None, None, None, None), P("grp"), P("grp"), P(), P(), P(), P())
    return jax.shard_map(
        body,
        mesh=mesh,
        in_specs=placed,
        out_specs=P(("grp", "tile"), None, None, None, None),
        check_vma=False,
    )
```

```python
import functools

import jax
import jax.numpy as jnp
from jax import lax
from jax.experimental import pallas as pl
from jax.experimental.pallas import tpu as pltpu
from jax.sharding import PartitionSpec as P

MESH = pl.DeviceIdType.MESH
F32 = jnp.float32
BF16 = jnp.bfloat16
GROUPS = 32
N = 32
ROWS = 32
COLS = 32
C = 512
CO = 256
CG = C // GROUPS
PER_VIDEO = 16
TX = 4
TY = 4
COUNT = float(TY * ROWS * TX * COLS * CG)
CHUNK = 16
EARLY = 0


def iota(shape, dim):
    return lax.broadcasted_iota(jnp.int32, shape, dim)


def thirds(x):
    high = x.astype(BF16).astype(F32)
    rest = x - high
    middle = rest.astype(BF16).astype(F32)
    return high, middle, rest - middle


def one_hot(mask):
    return jnp.where(mask, 1.0, 0.0).astype(BF16)


def dot(a, b):
    return jnp.dot(a, b, preferred_element_type=F32)


def activate(x, scale, offset):
    half = x * scale + offset
    return (half + half * jnp.tanh(half)).astype(BF16).astype(F32)


def kernel(
    lat_hbm, w_hbm, tos_hbm, len_hbm, tos_row_hbm, gain_hbm, shift_hbm, bias_hbm, out_ref,
    lat, w, wc, hp, acc, send1, recv1, send2, recv2, stat, srecv, norm, norm16, edge, pick, to_line, to_side,
    tos_s, len_s, tos_v, gain_ref, shift_ref, bias_ref,
    lat_sem, w_sem, small_sem, ssem, rsem,
):
    me = lax.axis_index("tile")
    grp = lax.axis_index("grp")
    my_x, my_z, my_core = me // 8, lax.rem(me // 2, 4), lax.rem(me, 2)

    def to_all(planes, action, fixed=False):
        xs = [8 * j if fixed else lax.rem(my_x + 2 + j, 4) * 8 for j in range(4)]
        for plane in planes:
            for x in xs:
                for core in (my_core, 1 - my_core):
                    to = x + plane * 2 + core
                    pl.when(to != me)(functools.partial(action, to))

    by_distance = (
        lax.rem(my_z + 2, 4), 3 - my_z, my_z + 1 - 2 * lax.rem(my_z, 2), my_z
    )
    barrier = pltpu.get_barrier_semaphore()

    def greet(to):
        pl.semaphore_signal(barrier, inc=1, device_id=(grp, to), device_id_type=MESH)

    to_all((by_distance[1], by_distance[0], by_distance[2], by_distance[3]), greet)
    lat_copies = [pltpu.make_async_copy(lat_hbm.at[f], lat.at[f], lat_sem.at[f]) for f in range(2)]
    for copy in lat_copies:
        copy.start()
    early_copy = pltpu.make_async_copy(w_hbm.at[0:18], w, w_sem.at[0])
    last_copy = pltpu.make_async_copy(w_hbm.at[18:27], wc.at[1], w_sem.at[1])

    small = [
        pltpu.make_async_copy(src, dst, small_sem.at[i])
        for i, (src, dst) in enumerate(
            (
                (tos_hbm, tos_s), (len_hbm, len_s), (tos_row_hbm, tos_v),
                (gain_hbm, gain_ref), (shift_hbm, shift_ref), (bias_hbm, bias_ref),
            )
        )
    ]
    for copy in small:
        copy.start()

    def send(phase, src, dst, to, slot=None):
        pltpu.make_async_remote_copy(
            src_ref=src, dst_ref=dst.at[me] if slot is None else dst.at[me, slot], send_sem=ssem.at[phase], recv_sem=rsem.at[phase],
            device_id=(grp, to), device_id_type=MESH,
        ).start()

    def whole(phase, dst):
        part = dst.at[pl.ds(0, N - 1)]
        return pltpu.make_async_remote_copy(
            src_ref=part, dst_ref=part, send_sem=ssem.at[phase], recv_sem=rsem.at[phase],
            device_id=(grp, lax.rem(me + 1, N)), device_id_type=MESH,
        )

    for copy in small:
        copy.wait()
    my_tile = tos_s[me]
    my_second = my_tile >= PER_VIDEO
    my_length = jnp.where(my_second, len_s[1], len_s[0])
    valid = [jnp.where(my_length > f, 1.0, 0.0).astype(F32) for f in range(2)]

    by_group = one_hot((iota((C, 128), 0) >> 4) == iota((C, 128), 1))
    total = jnp.zeros((1, C), F32)
    squares = jnp.zeros((1, C), F32)
    for f in range(2):
        lat_copies[f].wait()

        def row_sums(r, carry):
            s, q = carry
            x = lat[f, r].astype(F32)
            return s + x, q + x * x

        zero = jnp.zeros((COLS, C), F32)
        s, q = lax.fori_loop(0, ROWS, row_sums, (zero, zero))
        total = total + valid[f] * jnp.sum(s, axis=0, keepdims=True)
        squares = squares + valid[f] * jnp.sum(q, axis=0, keepdims=True)
    sub = iota((8, C), 0)
    early_copy.start()
    last_copy.start()
    six = jnp.zeros((8, C), F32)
    for i, row in enumerate((*thirds(total), *thirds(squares))):
        six = jnp.where(sub == i, jnp.broadcast_to(row, (8, C)), six)
    packed = dot(six.astype(BF16), by_group)
    stat[...] = packed[0:1] + packed[1:2] + packed[2:3] + pltpu.roll(
        packed[3:4] + packed[4:5] + packed[5:6], GROUPS, 1
    )

    def edge_rows(f, e, p):
        if e < 2:
            return lat[f, 0 if e == 0 else ROWS - 1, 8 * p : 8 * p + 8].astype(F32)
        found = jnp.zeros((8, C), F32)
        for q in range(8):
            if e == 2:
                block = lat[f, 8 * p + q, 0:16].astype(F32)[0:8]
                turned = pltpu.roll(block, q, 0) if q else block
            else:
                block = lat[f, 8 * p + q, 16:32].astype(F32)[8:16]
                turned = pltpu.roll(block, q + 1, 0) if q < 7 else block
            found = jnp.where(sub == q, turned, found)
        return found

    def quads(x, y):
        turned = pltpu.roll(x, 4, 0), pltpu.roll(y, 4, 0)
        top = sub[:, :128] < 4
        return jnp.where(top, x, turned[1]), jnp.where(top, turned[0], y)

    def lanes(x):
        return [x[:, 128 * q : 128 * (q + 1)] for q in range(4)]

    for f in range(2):
        for e in range(4):
            for p in range(4):
                q = lanes(edge_rows(f, e, p))
                front, back = quads(q[0], q[1]), quads(q[2], q[3])
                for i in range(2):
                    send1[f, e * 8 + 2 * p + i] = jnp.concatenate(
                        [front[i], back[i]], axis=0
                    ).astype(BF16)

    pl.semaphore_wait(barrier, N - 1)

    to_all(by_distance, lambda to: send(0, stat, srecv, to))
    to_all(by_distance, lambda to: send(1, send1.at[0, to], recv1.at[0], to))
    to_all(by_distance, lambda to: send(2, send1.at[1, to], recv1.at[1], to))
    srecv[me] = stat[...]
    for f in range(2):
        recv1[f, me] = send1[f, me]

    kind = me // 8
    part = lax.rem(me, 8)
    tos_row = tos_v[...].astype(F32)
    owner = iota((N * 8, N), 0) >> 3
    tile_here = jnp.sum(
        jnp.where(owner == iota((N * 8, N), 1), jnp.broadcast_to(tos_row, (N * 8, N)), 0.0),
        axis=1, keepdims=True,
    ).astype(jnp.int32)
    expand = one_hot(iota((N, N * 8), 0) == (iota((N, N * 8), 1) >> 2) & (N - 1))
    tile_there = dot(jnp.broadcast_to(tos_row, (8, N)).astype(BF16), expand)[0:1].astype(jnp.int32)
    row_step = jnp.where(kind == 0, 1, jnp.where(kind == 1, -1, 0))
    col_step = jnp.where(kind == 2, 1, jnp.where(kind == 3, -1, 0))
    line8 = iota((N * 8, 1), 0) & 7
    turn = jnp.where(kind < 2, 1, 100)
    low_end = jnp.where((line8 == 4) & (part == 0), turn, 0)
    high_end = jnp.where((line8 == 7) & (part == 7), turn, 0)
    near_row = ((tile_here & (PER_VIDEO - 1)) >> 2) + row_step
    near_col = (tile_here & (TX - 1)) + col_step + low_end - high_end
    inside = (near_row >= 0) & (near_row < TY) & (near_col >= 0) & (near_col < TX)
    near = jnp.where(
        inside, (tile_here & PER_VIDEO) + near_row * TX + near_col, -1
    )
    there = iota((N * 8, N * 8), 1)
    same_line = (iota((N * 8, N * 8), 0) & 7) == ((there >> 7) << 2) + (there & 3)
    pick[...] = jnp.where((near == tile_there) & same_line, 1.0, 0.0).astype(BF16)

    early_copy.wait()
    last_copy.wait()

    def add_weights(i, carry):
        tap, at = i // 4, pl.multiple_of(lax.rem(i, 4) * 128, 128)
        rows = pl.ds(at, 128)
        whole_sum = (
            w[tap, rows].astype(F32) + w[9 + tap, rows].astype(F32) + wc[1, tap, rows].astype(F32)
        )
        wc[0, tap, rows] = whole_sum.astype(BF16)
        return carry

    lax.fori_loop(0, 36, add_weights, 0)
    for u in range(2):
        hp[u, 0] = jnp.zeros((COLS, C), BF16)
        hp[u, ROWS + 1] = jnp.zeros((COLS, C), BF16)

    def hits(shape, half, pos):
        at = iota(shape, 1)
        g, r = at >> 4, at & 7
        lands = jnp.where(
            r < 4,
            4 * g + r,
            jnp.where(
                r == 4,
                (4 * g + 31) & 31,
                jnp.where(r == 7, (4 * g + 4) & 31, -1),
            ),
        )
        return (((at >> 3) & 1) == half) & (lands == pos)

    line_at = iota((64, 128), 0)
    to_line[...] = one_hot(hits((64, 128), line_at >> 5, line_at & 31))
    side_at = iota((512, 128), 0)
    on_side = hits((512, 128), side_at >> 8, (side_at & 255) >> 3)
    for i, edge_sub in enumerate((7, 0)):
        to_side[i] = one_hot(on_side & ((side_at & 7) == edge_sub))

    lane = iota((1, 128), 1)
    lane8, chan = iota((128, C), 0), iota((128, C), 1)
    to_channels = one_hot(((chan >> 4) == (lane8 & (GROUPS - 1))) & (lane8 < 3 * GROUPS))
    gain8 = jnp.broadcast_to(gain_ref[...] * 0.5, (8, C))
    shift8 = jnp.broadcast_to(shift_ref[...] * 0.5, (8, C))
    whole(0, srecv).wait_recv()
    sums = [jnp.zeros((1, 128), F32), jnp.zeros((1, 128), F32)]
    for s in range(N):
        row = srecv[s]
        second = jnp.where(tos_s[s] >= PER_VIDEO, 1.0, 0.0).astype(F32)
        sums = [sums[0] + row * (1.0 - second), sums[1] + row * second]
    four = jnp.zeros((8, 128), F32)
    for v in range(2):
        scaled = sums[v] / (len_s[v].astype(F32) * COUNT)
        mean = jnp.where(lane < GROUPS, scaled, 0.0)
        square = jnp.where(lane < GROUPS, pltpu.roll(scaled, 128 - GROUPS, 1), 0.0)
        inv = jnp.where(lane < GROUPS, 1.0 / jnp.sqrt(square - mean * mean + 1e-06), 0.0)
        for i, row in enumerate((mean, inv)):
            high, middle, low = thirds(row)
            row = high + pltpu.roll(middle, GROUPS, 1) + pltpu.roll(low, 2 * GROUPS, 1)
            four = jnp.where(sub[:, :128] == 2 * v + i, jnp.broadcast_to(row, (8, 128)), four)
    spread = dot(four.astype(BF16), to_channels)

    def fold(x):
        q = lanes(x)
        top = sub[:, :128] < 4
        return jnp.concatenate([jnp.where(top, q[0], q[1]), jnp.where(top, q[2], q[3])], axis=0)

    for v in range(2):
        mean = jnp.broadcast_to(spread[2 * v : 2 * v + 1], (8, C))
        scale = jnp.broadcast_to(spread[2 * v + 1 : 2 * v + 2], (8, C)) * gain8
        offset = shift8 - mean * scale
        norm[v, 0] = scale
        norm[v, 1] = offset
        norm16[v, 0] = fold(scale)
        norm16[v, 1] = fold(offset)

    mine = jnp.where(my_second, 1, 0)
    scale = jnp.concatenate([norm[mine, 0]] * 4, axis=0)
    offset = jnp.concatenate([norm[mine, 1]] * 4, axis=0)

    def hidden_row(r, carry):
        first = activate(lat[0, r].astype(F32), scale, offset)
        second = activate(lat[1, r].astype(F32), scale, offset)
        hp[0, r + 1] = first.astype(BF16)
        hp[1, r + 1] = (second - first).astype(BF16)
        return carry

    lax.fori_loop(0, ROWS, hidden_row, 0)
    col = iota((CHUNK * COLS, CO), 0) & (COLS - 1)

    def conv_rows(i, carry):
        per = ROWS // CHUNK
        u, r0 = lax.div(i, per), lax.rem(i, per) * CHUNK
        parts = []
        for c in range(3):
            part_sum = None
            for b in range(3):
                window = hp[u, pl.ds(r0 + b, CHUNK)].reshape(CHUNK * COLS, C)
                product = dot(window, wc[u, 3 * b + c])
                part_sum = product if part_sum is None else part_sum + product
            parts.append(part_sum)
        result = (
            parts[1]
            + jnp.where(col > 0, pltpu.roll(parts[0], 1, 0), 0.0)
            + jnp.where(col < COLS - 1, pltpu.roll(parts[2], CHUNK * COLS - 1, 0), 0.0)
        )
        acc[u, pl.ds(r0, CHUNK)] = result.reshape(CHUNK, COLS, CO)
        return carry

    if EARLY:
        lax.fori_loop(0, EARLY, conv_rows, 0)

    base = jnp.where(kind == 0, 6, jnp.where(kind == 2, 2, 0))
    stride = jnp.where(kind < 2, 1, 3)
    px = iota((N * 4, CO), 0) & 3

    for u in range(2):
        whole(1 + u, recv1.at[u]).wait_recv()

        def chunk_rows(i, carry):
            rows = []
            for j in range(2):
                pair = []
                for k in range(2):
                    s = 4 * i + 2 * j + k
                    v = jnp.where(tos_s[s] >= PER_VIDEO, 1, 0)
                    pair.append(
                        activate(recv1[u, s].astype(F32), norm16[v, 0], norm16[v, 1])
                    )
                front = quads(pair[0][:8], pair[1][:8])
                back = quads(pair[0][8:], pair[1][8:])
                rows.append(jnp.concatenate([*front, *back], axis=1))
            at = pl.ds(pl.multiple_of(16 * i, 16), 16)
            rows = jnp.concatenate(rows, axis=0)
            if u == 1:
                rows = rows - edge[0, at].astype(F32)
            edge[u, at] = rows.astype(BF16)
            return carry

        lax.fori_loop(0, N // 4, chunk_rows, 0, unroll=2)
        taps = []
        for t in range(3):
            tap = base + stride * t
            taps.append(dot(edge[u], wc[u, tap]))
        main = (
            taps[1]
            + jnp.where(px >= 1, pltpu.roll(taps[0], 1, 0), 0.0)
            + jnp.where(px <= 2, pltpu.roll(taps[2], N * 4 - 1, 0), 0.0)
        )
        extra = jnp.where(px == 3, taps[0], jnp.where(px == 0, taps[2], 0.0))
        both = jnp.concatenate([main, extra], axis=0).astype(BF16)
        picked = dot(pick[...], both).reshape(N, 8, CO)
        send2[:, u] = jnp.concatenate([picked[..., :128], picked[..., 128:]], axis=1).astype(BF16)
        to_all((0,), lambda to: send(3, send2.at[to, u], recv2, to, u), True)
        recv2[me, u] = send2[me, u]

    to_all((1, 2, 3), lambda to: send(3, send2.at[to], recv2, to), True)

    lax.fori_loop(EARLY, 2 * ROWS // CHUNK, conv_rows, 0)

    whole(3, recv2).wait_recv()

    def arrived(e):
        both = [recv2[8 * e : 8 * e + 8, u].reshape(128, 128) for u in range(2)]
        return jnp.concatenate(both, axis=1)

    for e, row in ((0, ROWS - 1), (1, 0)):
        line = dot(to_line[...], arrived(e))
        for u in range(2):
            for half in range(2):
                acc[u, row, :, 128 * half : 128 * half + 128] += line[
                    32 * half : 32 * half + 32, 128 * u : 128 * u + 128
                ]
    for e, at in ((2, COLS - 8), (3, 0)):
        side = dot(to_side[e - 2], arrived(e)).reshape(2, ROWS, 8, CO)
        for u in range(2):
            for half in range(2):
                acc[u, :, at : at + 8, 128 * half : 128 * half + 128] += side[
                    half, :, :, 128 * u : 128 * u + 128
                ]

    bias = jnp.broadcast_to(bias_ref[...], (COLS, CO))

    def finish(r, carry):
        first = acc[0, r] + bias
        out_ref[0, r] = (first * valid[0]).astype(BF16)
        out_ref[1, r] = ((first + acc[1, r]) * valid[1]).astype(BF16)
        return carry

    lax.fori_loop(0, ROWS, finish, 0)
    whole(0, srecv).wait_send()
    whole(3, recv2).wait_send()
    for u in range(2):
        whole(1 + u, recv1.at[u]).wait_send()


def body(latent, lengths, tile_of_slot, norm_gain, norm_shift, conv_weight, conv_bias):
    vmem = pl.BlockSpec(memory_space=pltpu.VMEM)
    hbm = pl.BlockSpec(memory_space=pltpu.HBM)
    decoded = pl.pallas_call(
        kernel,
        out_shape=jax.ShapeDtypeStruct((2, ROWS, COLS, CO), BF16),
        in_specs=[hbm] * 8,
        out_specs=vmem,
        scratch_shapes=[
            pltpu.VMEM((2, ROWS, COLS, C), BF16),
            pltpu.VMEM((18, C, CO), BF16),
            pltpu.VMEM((2, 9, C, CO), BF16),
            pltpu.VMEM((2, ROWS + 2, COLS, C), BF16),
            pltpu.VMEM((2, ROWS, COLS, CO), F32),
            pltpu.VMEM((2, N, 16, 128), BF16),
            pltpu.VMEM((2, N, 16, 128), BF16),
            pltpu.VMEM((N, 2, 16, 128), BF16),
            pltpu.VMEM((N, 2, 16, 128), BF16),
            pltpu.VMEM((1, 128), F32),
            pltpu.VMEM((N, 1, 128), F32),
            pltpu.VMEM((2, 2, 8, C), F32),
            pltpu.VMEM((2, 2, 16, 128), F32),
            pltpu.VMEM((2, N * 4, C), BF16),
            pltpu.VMEM((N * 8, N * 8), BF16),
            pltpu.VMEM((64, 128), BF16),
            pltpu.VMEM((2, 512, 128), BF16),
            pltpu.SMEM((N,), jnp.int32),
            pltpu.SMEM((2,), jnp.int32),
            pltpu.VMEM((1, N), jnp.int32),
            pltpu.VMEM((1, C), F32),
            pltpu.VMEM((1, C), F32),
            pltpu.VMEM((1, CO), F32),
            pltpu.SemaphoreType.DMA((2,)),
            pltpu.SemaphoreType.DMA((2,)),
            pltpu.SemaphoreType.DMA((6,)),
            pltpu.SemaphoreType.DMA((4,)),
            pltpu.SemaphoreType.DMA((4,)),
        ],
        compiler_params=pltpu.CompilerParams(
            collective_id=0, has_side_effects=True, vmem_limit_bytes=40 << 20
        ),
    )(
        *(
            pltpu.with_memory_space_constraint(x, pltpu.HBM)
            for x in (
                latent[0],
                conv_weight.reshape(27, C, CO),
                tile_of_slot,
                lengths,
                tile_of_slot.reshape(1, N),
                norm_gain.reshape(1, C),
                norm_shift.reshape(1, C),
                conv_bias.reshape(1, CO),
            )
        )
    )
    return decoded[None]


def solution(mesh):
    placed = (P(("grp", "tile"), None, None, None, None), P("grp"), P("grp"), P(), P(), P(), P())
    return jax.shard_map(
        body,
        mesh=mesh,
        in_specs=placed,
        out_specs=P(("grp", "tile"), None, None, None, None),
        check_vma=False,
    )
```

```python
import functools

import jax
import jax.numpy as jnp
from jax import lax
from jax.experimental import pallas as pl
from jax.experimental.pallas import tpu as pltpu
from jax.sharding import PartitionSpec as P

MESH = pl.DeviceIdType.MESH
F32 = jnp.float32
BF16 = jnp.bfloat16
GROUPS = 32
N = 32
ROWS = 32
COLS = 32
C = 512
CO = 256
CG = C // GROUPS
PER_VIDEO = 16
TX = 4
TY = 4
COUNT = float(TY * ROWS * TX * COLS * CG)
CHUNK = 16
EARLY = 0


def iota(shape, dim):
    return lax.broadcasted_iota(jnp.int32, shape, dim)


def thirds(x):
    high = x.astype(BF16).astype(F32)
    rest = x - high
    middle = rest.astype(BF16).astype(F32)
    return high, middle, rest - middle


def one_hot(mask):
    return jnp.where(mask, 1.0, 0.0).astype(BF16)


def dot(a, b):
    return jnp.dot(a, b, preferred_element_type=F32)


def activate(x, scale, offset):
    half = x * scale + offset
    return (half + half * jnp.tanh(half)).astype(BF16).astype(F32)


def kernel(
    lat_hbm, w_hbm, tos_hbm, len_hbm, tos_row_hbm, gain_hbm, shift_hbm, bias_hbm, out_ref,
    lat, w, wc, hp, acc, send1, recv1, send2, recv2, stat, srecv, norm, norm16, edge, pick, to_line, to_side,
    tos_s, len_s, tos_v, gain_ref, shift_ref, bias_ref,
    lat_sem, w_sem, small_sem, ssem, rsem,
):
    me = lax.axis_index("tile")
    grp = lax.axis_index("grp")
    my_x, my_z, my_core = me // 8, lax.rem(me // 2, 4), lax.rem(me, 2)

    def to_all(planes, action, fixed=False):
        xs = [8 * j if fixed else lax.rem(my_x + 2 + j, 4) * 8 for j in range(4)]
        for plane in planes:
            for x in xs:
                for core in (my_core, 1 - my_core):
                    to = x + plane * 2 + core
                    pl.when(to != me)(functools.partial(action, to))

    by_distance = (
        lax.rem(my_z + 2, 4), 3 - my_z, my_z + 1 - 2 * lax.rem(my_z, 2), my_z
    )
    barrier = pltpu.get_barrier_semaphore()

    def greet(to):
        pl.semaphore_signal(barrier, inc=1, device_id=(grp, to), device_id_type=MESH)

    to_all((by_distance[1], by_distance[0], by_distance[2], by_distance[3]), greet)
    lat_copies = [pltpu.make_async_copy(lat_hbm.at[f], lat.at[f], lat_sem.at[f]) for f in range(2)]
    for copy in lat_copies:
        copy.start()
    early_copy = pltpu.make_async_copy(w_hbm.at[0:18], w, w_sem.at[0])
    last_copy = pltpu.make_async_copy(w_hbm.at[18:27], wc.at[1], w_sem.at[1])

    small = [
        pltpu.make_async_copy(src, dst, small_sem.at[i])
        for i, (src, dst) in enumerate(
            (
                (tos_hbm, tos_s), (len_hbm, len_s), (tos_row_hbm, tos_v),
                (gain_hbm, gain_ref), (shift_hbm, shift_ref), (bias_hbm, bias_ref),
            )
        )
    ]
    for copy in small:
        copy.start()

    def send(phase, src, dst, to, slot=None):
        pltpu.make_async_remote_copy(
            src_ref=src, dst_ref=dst.at[me] if slot is None else dst.at[me, slot], send_sem=ssem.at[phase], recv_sem=rsem.at[phase],
            device_id=(grp, to), device_id_type=MESH,
        ).start()

    def whole(phase, dst):
        part = dst.at[pl.ds(0, N - 1)]
        return pltpu.make_async_remote_copy(
            src_ref=part, dst_ref=part, send_sem=ssem.at[phase], recv_sem=rsem.at[phase],
            device_id=(grp, lax.rem(me + 1, N)), device_id_type=MESH,
        )

    for copy in small:
        copy.wait()
    my_tile = tos_s[me]
    my_second = my_tile >= PER_VIDEO
    my_length = jnp.where(my_second, len_s[1], len_s[0])
    valid = [jnp.where(my_length > f, 1.0, 0.0).astype(F32) for f in range(2)]

    by_group = one_hot((iota((C, 128), 0) >> 4) == iota((C, 128), 1))
    total = jnp.zeros((1, C), F32)
    squares = jnp.zeros((1, C), F32)
    for f in range(2):
        lat_copies[f].wait()

        def row_sums(r, carry):
            s, q = carry
            x = lat[f, r].astype(F32)
            return s + x, q + x * x

        zero = jnp.zeros((COLS, C), F32)
        s, q = lax.fori_loop(0, ROWS, row_sums, (zero, zero))
        total = total + valid[f] * jnp.sum(s, axis=0, keepdims=True)
        squares = squares + valid[f] * jnp.sum(q, axis=0, keepdims=True)
    sub = iota((8, C), 0)
    early_copy.start()
    last_copy.start()
    six = jnp.zeros((8, C), F32)
    for i, row in enumerate((*thirds(total), *thirds(squares))):
        six = jnp.where(sub == i, jnp.broadcast_to(row, (8, C)), six)
    packed = dot(six.astype(BF16), by_group)
    stat[...] = packed[0:1] + packed[1:2] + packed[2:3] + pltpu.roll(
        packed[3:4] + packed[4:5] + packed[5:6], GROUPS, 1
    )

    def edge_rows(f, e, p):
        if e < 2:
            return lat[f, 0 if e == 0 else ROWS - 1, 8 * p : 8 * p + 8].astype(F32)
        found = jnp.zeros((8, C), F32)
        for q in range(8):
            if e == 2:
                block = lat[f, 8 * p + q, 0:16].astype(F32)[0:8]
                turned = pltpu.roll(block, q, 0) if q else block
            else:
                block = lat[f, 8 * p + q, 16:32].astype(F32)[8:16]
                turned = pltpu.roll(block, q + 1, 0) if q < 7 else block
            found = jnp.where(sub == q, turned, found)
        return found

    def quads(x, y):
        turned = pltpu.roll(x, 4, 0), pltpu.roll(y, 4, 0)
        top = sub[:, :128] < 4
        return jnp.where(top, x, turned[1]), jnp.where(top, turned[0], y)

    def lanes(x):
        return [x[:, 128 * q : 128 * (q + 1)] for q in range(4)]

    for f in range(2):
        for e in range(4):
            for p in range(4):
                q = lanes(edge_rows(f, e, p))
                front, back = quads(q[0], q[1]), quads(q[2], q[3])
                for i in range(2):
                    send1[f, e * 8 + 2 * p + i] = jnp.concatenate(
                        [front[i], back[i]], axis=0
                    ).astype(BF16)

    pl.semaphore_wait(barrier, N - 1)

    to_all(by_distance, lambda to: send(0, stat, srecv, to))
    to_all(by_distance, lambda to: send(1, send1.at[0, to], recv1.at[0], to))
    to_all(by_distance, lambda to: send(2, send1.at[1, to], recv1.at[1], to))
    srecv[me] = stat[...]
    for f in range(2):
        recv1[f, me] = send1[f, me]

    kind = me // 8
    part = lax.rem(me, 8)
    tos_row = tos_v[...].astype(F32)
    owner = iota((N * 8, N), 0) >> 3
    tile_here = jnp.sum(
        jnp.where(owner == iota((N * 8, N), 1), jnp.broadcast_to(tos_row, (N * 8, N)), 0.0),
        axis=1, keepdims=True,
    ).astype(jnp.int32)
    expand = one_hot(iota((N, N * 8), 0) == (iota((N, N * 8), 1) >> 2) & (N - 1))
    tile_there = dot(jnp.broadcast_to(tos_row, (8, N)).astype(BF16), expand)[0:1].astype(jnp.int32)
    row_step = jnp.where(kind == 0, 1, jnp.where(kind == 1, -1, 0))
    col_step = jnp.where(kind == 2, 1, jnp.where(kind == 3, -1, 0))
    line8 = iota((N * 8, 1), 0) & 7
    turn = jnp.where(kind < 2, 1, 100)
    low_end = jnp.where((line8 == 4) & (part == 0), turn, 0)
    high_end = jnp.where((line8 == 7) & (part == 7), turn, 0)
    near_row = ((tile_here & (PER_VIDEO - 1)) >> 2) + row_step
    near_col = (tile_here & (TX - 1)) + col_step + low_end - high_end
    inside = (near_row >= 0) & (near_row < TY) & (near_col >= 0) & (near_col < TX)
    near = jnp.where(
        inside, (tile_here & PER_VIDEO) + near_row * TX + near_col, -1
    )
    there = iota((N * 8, N * 8), 1)
    same_line = (iota((N * 8, N * 8), 0) & 7) == ((there >> 7) << 2) + (there & 3)
    pick[...] = jnp.where((near == tile_there) & same_line, 1.0, 0.0).astype(BF16)

    early_copy.wait()
    last_copy.wait()

    def add_weights(i, carry):
        tap, at = i // 4, pl.multiple_of(lax.rem(i, 4) * 128, 128)
        rows = pl.ds(at, 128)
        whole_sum = (
            w[tap, rows].astype(F32) + w[9 + tap, rows].astype(F32) + wc[1, tap, rows].astype(F32)
        )
        wc[0, tap, rows] = whole_sum.astype(BF16)
        return carry

    lax.fori_loop(0, 36, add_weights, 0)
    for u in range(2):
        hp[u, 0] = jnp.zeros((COLS, C), BF16)
        hp[u, ROWS + 1] = jnp.zeros((COLS, C), BF16)

    def hits(shape, half, pos):
        at = iota(shape, 1)
        g, r = at >> 4, at & 7
        lands = jnp.where(
            r < 4,
            4 * g + r,
            jnp.where(
                r == 4,
                (4 * g + 31) & 31,
                jnp.where(r == 7, (4 * g + 4) & 31, -1),
            ),
        )
        return (((at >> 3) & 1) == half) & (lands == pos)

    line_at = iota((64, 128), 0)
    to_line[...] = one_hot(hits((64, 128), line_at >> 5, line_at & 31))
    side_at = iota((512, 128), 0)
    on_side = hits((512, 128), side_at >> 8, (side_at & 255) >> 3)
    for i, edge_sub in enumerate((7, 0)):
        to_side[i] = one_hot(on_side & ((side_at & 7) == edge_sub))

    lane = iota((1, 128), 1)
    lane8, chan = iota((128, C), 0), iota((128, C), 1)
    to_channels = one_hot(((chan >> 4) == (lane8 & (GROUPS - 1))) & (lane8 < 3 * GROUPS))
    gain8 = jnp.broadcast_to(gain_ref[...] * 0.5, (8, C))
    shift8 = jnp.broadcast_to(shift_ref[...] * 0.5, (8, C))
    whole(0, srecv).wait_recv()
    sums = [jnp.zeros((1, 128), F32), jnp.zeros((1, 128), F32)]
    for s in range(N):
        row = srecv[s]
        second = jnp.where(tos_s[s] >= PER_VIDEO, 1.0, 0.0).astype(F32)
        sums = [sums[0] + row * (1.0 - second), sums[1] + row * second]
    four = jnp.zeros((8, 128), F32)
    for v in range(2):
        scaled = sums[v] / (len_s[v].astype(F32) * COUNT)
        mean = jnp.where(lane < GROUPS, scaled, 0.0)
        square = jnp.where(lane < GROUPS, pltpu.roll(scaled, 128 - GROUPS, 1), 0.0)
        inv = jnp.where(lane < GROUPS, 1.0 / jnp.sqrt(square - mean * mean + 1e-06), 0.0)
        for i, row in enumerate((mean, inv)):
            high, middle, low = thirds(row)
            row = high + pltpu.roll(middle, GROUPS, 1) + pltpu.roll(low, 2 * GROUPS, 1)
            four = jnp.where(sub[:, :128] == 2 * v + i, jnp.broadcast_to(row, (8, 128)), four)
    spread = dot(four.astype(BF16), to_channels)

    def fold(x):
        q = lanes(x)
        top = sub[:, :128] < 4
        return jnp.concatenate([jnp.where(top, q[0], q[1]), jnp.where(top, q[2], q[3])], axis=0)

    for v in range(2):
        mean = jnp.broadcast_to(spread[2 * v : 2 * v + 1], (8, C))
        scale = jnp.broadcast_to(spread[2 * v + 1 : 2 * v + 2], (8, C)) * gain8
        offset = shift8 - mean * scale
        norm[v, 0] = scale
        norm[v, 1] = offset
        norm16[v, 0] = fold(scale)
        norm16[v, 1] = fold(offset)

    mine = jnp.where(my_second, 1, 0)
    scale = jnp.concatenate([norm[mine, 0]] * 4, axis=0)
    offset = jnp.concatenate([norm[mine, 1]] * 4, axis=0)

    def hidden_row(r, carry):
        first = activate(lat[0, r].astype(F32), scale, offset)
        second = activate(lat[1, r].astype(F32), scale, offset)
        hp[0, r + 1] = first.astype(BF16)
        hp[1, r + 1] = (second - first).astype(BF16)
        return carry

    lax.fori_loop(0, ROWS, hidden_row, 0)
    col = iota((CHUNK * COLS, CO), 0) & (COLS - 1)

    def conv_rows(i, carry):
        per = ROWS // CHUNK
        u, r0 = lax.div(i, per), lax.rem(i, per) * CHUNK
        parts = []
        for c in range(3):
            part_sum = None
            for b in range(3):
                window = hp[u, pl.ds(r0 + b, CHUNK)].reshape(CHUNK * COLS, C)
                product = dot(window, wc[u, 3 * b + c])
                part_sum = product if part_sum is None else part_sum + product
            parts.append(part_sum)
        result = (
            parts[1]
            + jnp.where(col > 0, pltpu.roll(parts[0], 1, 0), 0.0)
            + jnp.where(col < COLS - 1, pltpu.roll(parts[2], CHUNK * COLS - 1, 0), 0.0)
        )
        acc[u, pl.ds(r0, CHUNK)] = result.reshape(CHUNK, COLS, CO)
        return carry

    if EARLY:
        lax.fori_loop(0, EARLY, conv_rows, 0)

    base = jnp.where(kind == 0, 6, jnp.where(kind == 2, 2, 0))
    stride = jnp.where(kind < 2, 1, 3)
    px = iota((N * 4, CO), 0) & 3

    for u in range(2):
        whole(1 + u, recv1.at[u]).wait_recv()

        def chunk_rows(i, carry):
            rows = []
            for j in range(2):
                pair = []
                for k in range(2):
                    s = 4 * i + 2 * j + k
                    v = jnp.where(tos_s[s] >= PER_VIDEO, 1, 0)
                    pair.append(
                        activate(recv1[u, s].astype(F32), norm16[v, 0], norm16[v, 1])
                    )
                front = quads(pair[0][:8], pair[1][:8])
                back = quads(pair[0][8:], pair[1][8:])
                rows.append(jnp.concatenate([*front, *back], axis=1))
            at = pl.ds(pl.multiple_of(16 * i, 16), 16)
            rows = jnp.concatenate(rows, axis=0)
            if u == 1:
                rows = rows - edge[0, at].astype(F32)
            edge[u, at] = rows.astype(BF16)
            return carry

        lax.fori_loop(0, N // 4, chunk_rows, 0, unroll=2)
        taps = []
        for t in range(3):
            tap = base + stride * t
            taps.append(dot(edge[u], wc[u, tap]))
        main = (
            taps[1]
            + jnp.where(px >= 1, pltpu.roll(taps[0], 1, 0), 0.0)
            + jnp.where(px <= 2, pltpu.roll(taps[2], N * 4 - 1, 0), 0.0)
        )
        extra = jnp.where(px == 3, taps[0], jnp.where(px == 0, taps[2], 0.0))
        both = jnp.concatenate([main, extra], axis=0).astype(BF16)
        picked = dot(pick[...], both).reshape(N, 8, CO)
        send2[:, u] = jnp.concatenate([picked[..., :128], picked[..., 128:]], axis=1).astype(BF16)
        to_all((0,), lambda to: send(3, send2.at[to, u], recv2, to, u), True)
        recv2[me, u] = send2[me, u]

    to_all((1, 2, 3), lambda to: send(3, send2.at[to], recv2, to), True)

    lax.fori_loop(EARLY, 2 * ROWS // CHUNK, conv_rows, 0)

    def finish_part(r, at, count):
        cols = pl.ds(at, count)
        first = acc[0, r, cols] + bias_ref[...]
        out_ref[0, r, cols] = (first * valid[0]).astype(BF16)
        out_ref[1, r, cols] = ((first + acc[1, r, cols]) * valid[1]).astype(BF16)

    def finish(r, carry):
        finish_part(r, 0, COLS)
        return carry

    def finish_sides(r, carry):
        finish_part(r, 0, 8)
        finish_part(r, COLS - 8, 8)
        return carry

    lax.fori_loop(0, ROWS, finish, 0)

    whole(3, recv2).wait_recv()

    def arrived(e):
        both = [recv2[8 * e : 8 * e + 8, u].reshape(128, 128) for u in range(2)]
        return jnp.concatenate(both, axis=1)

    for e, row in ((0, ROWS - 1), (1, 0)):
        line = dot(to_line[...], arrived(e))
        for u in range(2):
            for half in range(2):
                acc[u, row, :, 128 * half : 128 * half + 128] += line[
                    32 * half : 32 * half + 32, 128 * u : 128 * u + 128
                ]
    for e, at in ((2, COLS - 8), (3, 0)):
        side = dot(to_side[e - 2], arrived(e)).reshape(2, ROWS, 8, CO)
        for u in range(2):
            for half in range(2):
                acc[u, :, at : at + 8, 128 * half : 128 * half + 128] += side[
                    half, :, :, 128 * u : 128 * u + 128
                ]

    lax.fori_loop(0, ROWS, finish_sides, 0)
    finish(0, 0)
    finish(ROWS - 1, 0)
    whole(0, srecv).wait_send()
    whole(3, recv2).wait_send()
    for u in range(2):
        whole(1 + u, recv1.at[u]).wait_send()


def body(latent, lengths, tile_of_slot, norm_gain, norm_shift, conv_weight, conv_bias):
    vmem = pl.BlockSpec(memory_space=pltpu.VMEM)
    hbm = pl.BlockSpec(memory_space=pltpu.HBM)
    decoded = pl.pallas_call(
        kernel,
        out_shape=jax.ShapeDtypeStruct((2, ROWS, COLS, CO), BF16),
        in_specs=[hbm] * 8,
        out_specs=vmem,
        scratch_shapes=[
            pltpu.VMEM((2, ROWS, COLS, C), BF16),
            pltpu.VMEM((18, C, CO), BF16),
            pltpu.VMEM((2, 9, C, CO), BF16),
            pltpu.VMEM((2, ROWS + 2, COLS, C), BF16),
            pltpu.VMEM((2, ROWS, COLS, CO), F32),
            pltpu.VMEM((2, N, 16, 128), BF16),
            pltpu.VMEM((2, N, 16, 128), BF16),
            pltpu.VMEM((N, 2, 16, 128), BF16),
            pltpu.VMEM((N, 2, 16, 128), BF16),
            pltpu.VMEM((1, 128), F32),
            pltpu.VMEM((N, 1, 128), F32),
            pltpu.VMEM((2, 2, 8, C), F32),
            pltpu.VMEM((2, 2, 16, 128), F32),
            pltpu.VMEM((2, N * 4, C), BF16),
            pltpu.VMEM((N * 8, N * 8), BF16),
            pltpu.VMEM((64, 128), BF16),
            pltpu.VMEM((2, 512, 128), BF16),
            pltpu.SMEM((N,), jnp.int32),
            pltpu.SMEM((2,), jnp.int32),
            pltpu.VMEM((1, N), jnp.int32),
            pltpu.VMEM((1, C), F32),
            pltpu.VMEM((1, C), F32),
            pltpu.VMEM((1, CO), F32),
            pltpu.SemaphoreType.DMA((2,)),
            pltpu.SemaphoreType.DMA((2,)),
            pltpu.SemaphoreType.DMA((6,)),
            pltpu.SemaphoreType.DMA((4,)),
            pltpu.SemaphoreType.DMA((4,)),
        ],
        compiler_params=pltpu.CompilerParams(
            collective_id=0, has_side_effects=True, vmem_limit_bytes=40 << 20
        ),
    )(
        *(
            pltpu.with_memory_space_constraint(x, pltpu.HBM)
            for x in (
                latent[0],
                conv_weight.reshape(27, C, CO),
                tile_of_slot,
                lengths,
                tile_of_slot.reshape(1, N),
                norm_gain.reshape(1, C),
                norm_shift.reshape(1, C),
                conv_bias.reshape(1, CO),
            )
        )
    )
    return decoded[None]


def solution(mesh):
    placed = (P(("grp", "tile"), None, None, None, None), P("grp"), P("grp"), P(), P(), P(), P())
    return jax.shard_map(
        body,
        mesh=mesh,
        in_specs=placed,
        out_specs=P(("grp", "tile"), None, None, None, None),
        check_vma=False,
    )
```

```python
import functools

import jax
import jax.numpy as jnp
from jax import lax
from jax.experimental import pallas as pl
from jax.experimental.pallas import tpu as pltpu
from jax.sharding import PartitionSpec as P

MESH = pl.DeviceIdType.MESH
F32 = jnp.float32
BF16 = jnp.bfloat16
GROUPS = 32
N = 32
ROWS = 32
COLS = 32
C = 512
CO = 256
CG = C // GROUPS
PER_VIDEO = 16
TX = 4
TY = 4
COUNT = float(TY * ROWS * TX * COLS * CG)
CHUNK = 32
EARLY = 0


def iota(shape, dim):
    return lax.broadcasted_iota(jnp.int32, shape, dim)


def thirds(x):
    high = x.astype(BF16).astype(F32)
    rest = x - high
    middle = rest.astype(BF16).astype(F32)
    return high, middle, rest - middle


def one_hot(mask):
    return jnp.where(mask, 1.0, 0.0).astype(BF16)


def dot(a, b):
    return jnp.dot(a, b, preferred_element_type=F32)


def activate(x, scale, offset):
    half = x * scale + offset
    return (half + half * jnp.tanh(half)).astype(BF16).astype(F32)


def kernel(
    lat_hbm, w_hbm, tos_hbm, len_hbm, tos_row_hbm, gain_hbm, shift_hbm, bias_hbm, out_ref,
    lat, w, wc, hp, acc, send1, recv1, send2, recv2, stat, srecv, norm, norm16, edge, pick, to_line, to_side,
    tos_s, len_s, tos_v, gain_ref, shift_ref, bias_ref,
    lat_sem, w_sem, small_sem, ssem, rsem,
):
    me = lax.axis_index("tile")
    grp = lax.axis_index("grp")
    my_x, my_z, my_core = me // 8, lax.rem(me // 2, 4), lax.rem(me, 2)

    def to_all(planes, action, fixed=False):
        xs = [8 * j if fixed else lax.rem(my_x + 2 + j, 4) * 8 for j in range(4)]
        for plane in planes:
            for x in xs:
                for core in (my_core, 1 - my_core):
                    to = x + plane * 2 + core
                    pl.when(to != me)(functools.partial(action, to))

    by_distance = (
        lax.rem(my_z + 2, 4), 3 - my_z, my_z + 1 - 2 * lax.rem(my_z, 2), my_z
    )
    barrier = pltpu.get_barrier_semaphore()

    def greet(to):
        pl.semaphore_signal(barrier, inc=1, device_id=(grp, to), device_id_type=MESH)

    to_all((by_distance[1], by_distance[0], by_distance[2], by_distance[3]), greet)
    lat_copies = [pltpu.make_async_copy(lat_hbm.at[f], lat.at[f], lat_sem.at[f]) for f in range(2)]
    for copy in lat_copies:
        copy.start()
    early_copy = pltpu.make_async_copy(w_hbm.at[0:18], w, w_sem.at[0])
    last_copy = pltpu.make_async_copy(w_hbm.at[18:27], wc.at[1], w_sem.at[1])

    small = [
        pltpu.make_async_copy(src, dst, small_sem.at[i])
        for i, (src, dst) in enumerate(
            (
                (tos_hbm, tos_s), (len_hbm, len_s), (tos_row_hbm, tos_v),
                (gain_hbm, gain_ref), (shift_hbm, shift_ref), (bias_hbm, bias_ref),
            )
        )
    ]
    for copy in small:
        copy.start()

    def send(phase, src, dst, to, slot=None):
        pltpu.make_async_remote_copy(
            src_ref=src, dst_ref=dst.at[me] if slot is None else dst.at[me, slot], send_sem=ssem.at[phase], recv_sem=rsem.at[phase],
            device_id=(grp, to), device_id_type=MESH,
        ).start()

    def whole(phase, dst):
        part = dst.at[pl.ds(0, N - 1)]
        return pltpu.make_async_remote_copy(
            src_ref=part, dst_ref=part, send_sem=ssem.at[phase], recv_sem=rsem.at[phase],
            device_id=(grp, lax.rem(me + 1, N)), device_id_type=MESH,
        )

    for copy in small:
        copy.wait()
    my_tile = tos_s[me]
    my_second = my_tile >= PER_VIDEO
    my_length = jnp.where(my_second, len_s[1], len_s[0])
    valid = [jnp.where(my_length > f, 1.0, 0.0).astype(F32) for f in range(2)]

    by_group = one_hot((iota((C, 128), 0) >> 4) == iota((C, 128), 1))
    total = jnp.zeros((1, C), F32)
    squares = jnp.zeros((1, C), F32)
    for f in range(2):
        lat_copies[f].wait()

        def row_sums(r, carry):
            s, q = carry
            x = lat[f, r].astype(F32)
            return s + x, q + x * x

        zero = jnp.zeros((COLS, C), F32)
        s, q = lax.fori_loop(0, ROWS, row_sums, (zero, zero))
        total = total + valid[f] * jnp.sum(s, axis=0, keepdims=True)
        squares = squares + valid[f] * jnp.sum(q, axis=0, keepdims=True)
    sub = iota((8, C), 0)
    early_copy.start()
    last_copy.start()
    six = jnp.zeros((8, C), F32)
    for i, row in enumerate((*thirds(total), *thirds(squares))):
        six = jnp.where(sub == i, jnp.broadcast_to(row, (8, C)), six)
    packed = dot(six.astype(BF16), by_group)
    stat[...] = packed[0:1] + packed[1:2] + packed[2:3] + pltpu.roll(
        packed[3:4] + packed[4:5] + packed[5:6], GROUPS, 1
    )

    def edge_rows(f, e, p):
        if e < 2:
            return lat[f, 0 if e == 0 else ROWS - 1, 8 * p : 8 * p + 8].astype(F32)
        found = jnp.zeros((8, C), F32)
        for q in range(8):
            if e == 2:
                block = lat[f, 8 * p + q, 0:16].astype(F32)[0:8]
                turned = pltpu.roll(block, q, 0) if q else block
            else:
                block = lat[f, 8 * p + q, 16:32].astype(F32)[8:16]
                turned = pltpu.roll(block, q + 1, 0) if q < 7 else block
            found = jnp.where(sub == q, turned, found)
        return found

    def quads(x, y):
        turned = pltpu.roll(x, 4, 0), pltpu.roll(y, 4, 0)
        top = sub[:, :128] < 4
        return jnp.where(top, x, turned[1]), jnp.where(top, turned[0], y)

    def lanes(x):
        return [x[:, 128 * q : 128 * (q + 1)] for q in range(4)]

    for f in range(2):
        for e in range(4):
            for p in range(4):
                q = lanes(edge_rows(f, e, p))
                front, back = quads(q[0], q[1]), quads(q[2], q[3])
                for i in range(2):
                    send1[f, e * 8 + 2 * p + i] = jnp.concatenate(
                        [front[i], back[i]], axis=0
                    ).astype(BF16)

    pl.semaphore_wait(barrier, N - 1)

    to_all(by_distance, lambda to: send(0, stat, srecv, to))
    to_all(by_distance, lambda to: send(1, send1.at[0, to], recv1.at[0], to))
    to_all(by_distance, lambda to: send(2, send1.at[1, to], recv1.at[1], to))
    srecv[me] = stat[...]
    for f in range(2):
        recv1[f, me] = send1[f, me]

    kind = me // 8
    part = lax.rem(me, 8)
    tos_row = tos_v[...].astype(F32)
    owner = iota((N * 8, N), 0) >> 3
    tile_here = jnp.sum(
        jnp.where(owner == iota((N * 8, N), 1), jnp.broadcast_to(tos_row, (N * 8, N)), 0.0),
        axis=1, keepdims=True,
    ).astype(jnp.int32)
    expand = one_hot(iota((N, N * 8), 0) == (iota((N, N * 8), 1) >> 2) & (N - 1))
    tile_there = dot(jnp.broadcast_to(tos_row, (8, N)).astype(BF16), expand)[0:1].astype(jnp.int32)
    row_step = jnp.where(kind == 0, 1, jnp.where(kind == 1, -1, 0))
    col_step = jnp.where(kind == 2, 1, jnp.where(kind == 3, -1, 0))
    line8 = iota((N * 8, 1), 0) & 7
    turn = jnp.where(kind < 2, 1, 100)
    low_end = jnp.where((line8 == 4) & (part == 0), turn, 0)
    high_end = jnp.where((line8 == 7) & (part == 7), turn, 0)
    near_row = ((tile_here & (PER_VIDEO - 1)) >> 2) + row_step
    near_col = (tile_here & (TX - 1)) + col_step + low_end - high_end
    inside = (near_row >= 0) & (near_row < TY) & (near_col >= 0) & (near_col < TX)
    near = jnp.where(
        inside, (tile_here & PER_VIDEO) + near_row * TX + near_col, -1
    )
    there = iota((N * 8, N * 8), 1)
    same_line = (iota((N * 8, N * 8), 0) & 7) == ((there >> 7) << 2) + (there & 3)
    pick[...] = jnp.where((near == tile_there) & same_line, 1.0, 0.0).astype(BF16)

    early_copy.wait()
    last_copy.wait()

    def add_weights(i, carry):
        tap, at = i // 4, pl.multiple_of(lax.rem(i, 4) * 128, 128)
        rows = pl.ds(at, 128)
        whole_sum = (
            w[tap, rows].astype(F32) + w[9 + tap, rows].astype(F32) + wc[1, tap, rows].astype(F32)
        )
        wc[0, tap, rows] = whole_sum.astype(BF16)
        return carry

    lax.fori_loop(0, 36, add_weights, 0)
    for u in range(2):
        hp[u, 0] = jnp.zeros((COLS, C), BF16)
        hp[u, ROWS + 1] = jnp.zeros((COLS, C), BF16)

    def hits(shape, half, pos):
        at = iota(shape, 1)
        g, r = at >> 4, at & 7
        lands = jnp.where(
            r < 4,
            4 * g + r,
            jnp.where(
                r == 4,
                (4 * g + 31) & 31,
                jnp.where(r == 7, (4 * g + 4) & 31, -1),
            ),
        )
        return (((at >> 3) & 1) == half) & (lands == pos)

    line_at = iota((64, 128), 0)
    to_line[...] = one_hot(hits((64, 128), line_at >> 5, line_at & 31))
    side_at = iota((512, 128), 0)
    on_side = hits((512, 128), side_at >> 8, (side_at & 255) >> 3)
    for i, edge_sub in enumerate((7, 0)):
        to_side[i] = one_hot(on_side & ((side_at & 7) == edge_sub))

    lane = iota((1, 128), 1)
    lane8, chan = iota((128, C), 0), iota((128, C), 1)
    to_channels = one_hot(((chan >> 4) == (lane8 & (GROUPS - 1))) & (lane8 < 3 * GROUPS))
    gain8 = jnp.broadcast_to(gain_ref[...] * 0.5, (8, C))
    shift8 = jnp.broadcast_to(shift_ref[...] * 0.5, (8, C))
    whole(0, srecv).wait_recv()
    sums = [jnp.zeros((1, 128), F32), jnp.zeros((1, 128), F32)]
    for s in range(N):
        row = srecv[s]
        second = jnp.where(tos_s[s] >= PER_VIDEO, 1.0, 0.0).astype(F32)
        sums = [sums[0] + row * (1.0 - second), sums[1] + row * second]
    four = jnp.zeros((8, 128), F32)
    for v in range(2):
        scaled = sums[v] / (len_s[v].astype(F32) * COUNT)
        mean = jnp.where(lane < GROUPS, scaled, 0.0)
        square = jnp.where(lane < GROUPS, pltpu.roll(scaled, 128 - GROUPS, 1), 0.0)
        inv = jnp.where(lane < GROUPS, 1.0 / jnp.sqrt(square - mean * mean + 1e-06), 0.0)
        for i, row in enumerate((mean, inv)):
            high, middle, low = thirds(row)
            row = high + pltpu.roll(middle, GROUPS, 1) + pltpu.roll(low, 2 * GROUPS, 1)
            four = jnp.where(sub[:, :128] == 2 * v + i, jnp.broadcast_to(row, (8, 128)), four)
    spread = dot(four.astype(BF16), to_channels)

    def fold(x):
        q = lanes(x)
        top = sub[:, :128] < 4
        return jnp.concatenate([jnp.where(top, q[0], q[1]), jnp.where(top, q[2], q[3])], axis=0)

    for v in range(2):
        mean = jnp.broadcast_to(spread[2 * v : 2 * v + 1], (8, C))
        scale = jnp.broadcast_to(spread[2 * v + 1 : 2 * v + 2], (8, C)) * gain8
        offset = shift8 - mean * scale
        norm[v, 0] = scale
        norm[v, 1] = offset
        norm16[v, 0] = fold(scale)
        norm16[v, 1] = fold(offset)

    mine = jnp.where(my_second, 1, 0)
    scale = jnp.concatenate([norm[mine, 0]] * 4, axis=0)
    offset = jnp.concatenate([norm[mine, 1]] * 4, axis=0)

    def hidden_row(r, carry):
        first = activate(lat[0, r].astype(F32), scale, offset)
        second = activate(lat[1, r].astype(F32), scale, offset)
        hp[0, r + 1] = first.astype(BF16)
        hp[1, r + 1] = (second - first).astype(BF16)
        return carry

    lax.fori_loop(0, ROWS, hidden_row, 0)
    col = iota((CHUNK * COLS, CO), 0) & (COLS - 1)

    def conv_rows(i, carry):
        per = ROWS // CHUNK
        u, r0 = lax.div(i, per), lax.rem(i, per) * CHUNK
        parts = []
        for c in range(3):
            part_sum = None
            for b in range(3):
                window = hp[u, pl.ds(r0 + b, CHUNK)].reshape(CHUNK * COLS, C)
                product = dot(window, wc[u, 3 * b + c])
                part_sum = product if part_sum is None else part_sum + product
            parts.append(part_sum)
        result = (
            parts[1]
            + jnp.where(col > 0, pltpu.roll(parts[0], 1, 0), 0.0)
            + jnp.where(col < COLS - 1, pltpu.roll(parts[2], CHUNK * COLS - 1, 0), 0.0)
        )
        acc[u, pl.ds(r0, CHUNK)] = result.reshape(CHUNK, COLS, CO)
        return carry

    if EARLY:
        lax.fori_loop(0, EARLY, conv_rows, 0)

    base = jnp.where(kind == 0, 6, jnp.where(kind == 2, 2, 0))
    stride = jnp.where(kind < 2, 1, 3)
    px = iota((N * 4, CO), 0) & 3

    for u in range(2):
        whole(1 + u, recv1.at[u]).wait_recv()

        def chunk_rows(i, carry):
            rows = []
            for j in range(2):
                pair = []
                for k in range(2):
                    s = 4 * i + 2 * j + k
                    v = jnp.where(tos_s[s] >= PER_VIDEO, 1, 0)
                    pair.append(
                        activate(recv1[u, s].astype(F32), norm16[v, 0], norm16[v, 1])
                    )
                front = quads(pair[0][:8], pair[1][:8])
                back = quads(pair[0][8:], pair[1][8:])
                rows.append(jnp.concatenate([*front, *back], axis=1))
            at = pl.ds(pl.multiple_of(16 * i, 16), 16)
            rows = jnp.concatenate(rows, axis=0)
            if u == 1:
                rows = rows - edge[0, at].astype(F32)
            edge[u, at] = rows.astype(BF16)
            return carry

        lax.fori_loop(0, N // 4, chunk_rows, 0, unroll=2)
        taps = []
        for t in range(3):
            tap = base + stride * t
            taps.append(dot(edge[u], wc[u, tap]))
        main = (
            taps[1]
            + jnp.where(px >= 1, pltpu.roll(taps[0], 1, 0), 0.0)
            + jnp.where(px <= 2, pltpu.roll(taps[2], N * 4 - 1, 0), 0.0)
        )
        extra = jnp.where(px == 3, taps[0], jnp.where(px == 0, taps[2], 0.0))
        both = jnp.concatenate([main, extra], axis=0).astype(BF16)
        picked = dot(pick[...], both).reshape(N, 8, CO)
        send2[:, u] = jnp.concatenate([picked[..., :128], picked[..., 128:]], axis=1).astype(BF16)
        to_all((0,), lambda to: send(3, send2.at[to, u], recv2, to, u), True)
        recv2[me, u] = send2[me, u]

    to_all((1, 2, 3), lambda to: send(3, send2.at[to], recv2, to), True)

    lax.fori_loop(EARLY, 2 * ROWS // CHUNK, conv_rows, 0)

    def finish_part(r, at, count):
        cols = pl.ds(at, count)
        first = acc[0, r, cols] + bias_ref[...]
        out_ref[0, r, cols] = (first * valid[0]).astype(BF16)
        out_ref[1, r, cols] = ((first + acc[1, r, cols]) * valid[1]).astype(BF16)

    def finish(r, carry):
        finish_part(r, 0, COLS)
        return carry

    def finish_sides(r, carry):
        finish_part(r, 0, 8)
        finish_part(r, COLS - 8, 8)
        return carry

    lax.fori_loop(0, ROWS, finish, 0)

    whole(3, recv2).wait_recv()

    def arrived(e):
        both = [recv2[8 * e : 8 * e + 8, u].reshape(128, 128) for u in range(2)]
        return jnp.concatenate(both, axis=1)

    for e, row in ((0, ROWS - 1), (1, 0)):
        line = dot(to_line[...], arrived(e))
        for u in range(2):
            for half in range(2):
                acc[u, row, :, 128 * half : 128 * half + 128] += line[
                    32 * half : 32 * half + 32, 128 * u : 128 * u + 128
                ]
    for e, at in ((2, COLS - 8), (3, 0)):
        side = dot(to_side[e - 2], arrived(e)).reshape(2, ROWS, 8, CO)
        for u in range(2):
            for half in range(2):
                acc[u, :, at : at + 8, 128 * half : 128 * half + 128] += side[
                    half, :, :, 128 * u : 128 * u + 128
                ]

    lax.fori_loop(0, ROWS, finish_sides, 0)
    finish(0, 0)
    finish(ROWS - 1, 0)
    whole(0, srecv).wait_send()
    whole(3, recv2).wait_send()
    for u in range(2):
        whole(1 + u, recv1.at[u]).wait_send()


def body(latent, lengths, tile_of_slot, norm_gain, norm_shift, conv_weight, conv_bias):
    vmem = pl.BlockSpec(memory_space=pltpu.VMEM)
    hbm = pl.BlockSpec(memory_space=pltpu.HBM)
    decoded = pl.pallas_call(
        kernel,
        out_shape=jax.ShapeDtypeStruct((2, ROWS, COLS, CO), BF16),
        in_specs=[hbm] * 8,
        out_specs=vmem,
        scratch_shapes=[
            pltpu.VMEM((2, ROWS, COLS, C), BF16),
            pltpu.VMEM((18, C, CO), BF16),
            pltpu.VMEM((2, 9, C, CO), BF16),
            pltpu.VMEM((2, ROWS + 2, COLS, C), BF16),
            pltpu.VMEM((2, ROWS, COLS, CO), F32),
            pltpu.VMEM((2, N, 16, 128), BF16),
            pltpu.VMEM((2, N, 16, 128), BF16),
            pltpu.VMEM((N, 2, 16, 128), BF16),
            pltpu.VMEM((N, 2, 16, 128), BF16),
            pltpu.VMEM((1, 128), F32),
            pltpu.VMEM((N, 1, 128), F32),
            pltpu.VMEM((2, 2, 8, C), F32),
            pltpu.VMEM((2, 2, 16, 128), F32),
            pltpu.VMEM((2, N * 4, C), BF16),
            pltpu.VMEM((N * 8, N * 8), BF16),
            pltpu.VMEM((64, 128), BF16),
            pltpu.VMEM((2, 512, 128), BF16),
            pltpu.SMEM((N,), jnp.int32),
            pltpu.SMEM((2,), jnp.int32),
            pltpu.VMEM((1, N), jnp.int32),
            pltpu.VMEM((1, C), F32),
            pltpu.VMEM((1, C), F32),
            pltpu.VMEM((1, CO), F32),
            pltpu.SemaphoreType.DMA((2,)),
            pltpu.SemaphoreType.DMA((2,)),
            pltpu.SemaphoreType.DMA((6,)),
            pltpu.SemaphoreType.DMA((4,)),
            pltpu.SemaphoreType.DMA((4,)),
        ],
        compiler_params=pltpu.CompilerParams(
            collective_id=0, has_side_effects=True, vmem_limit_bytes=40 << 20
        ),
    )(
        *(
            pltpu.with_memory_space_constraint(x, pltpu.HBM)
            for x in (
                latent[0],
                conv_weight.reshape(27, C, CO),
                tile_of_slot,
                lengths,
                tile_of_slot.reshape(1, N),
                norm_gain.reshape(1, C),
                norm_shift.reshape(1, C),
                conv_bias.reshape(1, CO),
            )
        )
    )
    return decoded[None]


def solution(mesh):
    placed = (P(("grp", "tile"), None, None, None, None), P("grp"), P("grp"), P(), P(), P(), P())
    return jax.shard_map(
        body,
        mesh=mesh,
        in_specs=placed,
        out_specs=P(("grp", "tile"), None, None, None, None),
        check_vma=False,
    )
```
